32 devices in a mesh: dp: 8 (over z, y), blk: 4 (over x, core).
Axes of the slice: x: 2, y: 2, z: 4, core: 2. Of those that a mesh axis runs over, the one named last changes fastest.
Arguments:
- tokens: bfloat16 [2, 16, 256, 512], P(None, 'dp', 'blk'), may hold values from -6 to 6
- mask_flags: int32 [2, 16, 256], P(None, 'dp', 'blk'), may hold values 0 or 1
- buckets: int32 [2, 8], P(None, 'dp'), may hold values from 0 to 2
- cotangent: bfloat16 [2, 16, 256, 512], P(None, 'dp', 'blk'), may hold values from -6 to 6
- mask_token: bfloat16 [512], replicated, may hold values from -5 to 5
- norm1_gain: bfloat16 [512], replicated, may hold values from 0.5 to 1.5
- norm1_bias: bfloat16 [512], replicated, may hold values from -1.5 to 1.5
- w_qkv: bfloat16 [512, 1536], replicated, may hold values from -0.25 to 0.25
- b_query: bfloat16 [512], replicated, may hold values from -1.5 to 1.5
- b_value: bfloat16 [512], replicated, may hold values from -1.5 to 1.5
- w_out: bfloat16 [512, 512], replicated, may hold values from -1 to 1
- b_out: bfloat16 [512], replicated, may hold values from -1.5 to 1.5
- norm2_gain: bfloat16 [512], replicated, may hold values from 0.5 to 1.5
- norm2_bias: bfloat16 [512], replicated, may hold values from -1.5 to 1.5
- w_up: bfloat16 [512, 2048], replicated, may hold values from -0.25 to 0.25
- b_up: bfloat16 [2048], replicated, may hold values from -1.5 to 1.5
- w_down: bfloat16 [2048, 512], replicated, may hold values from -0.125 to 0.125
- b_down: bfloat16 [512], replicated, may hold values from -1.5 to 1.5
Outputs:
- block_out: bfloat16 [2, 16, 256, 512], P(None, 'dp', 'blk')
- token_grad: float32 [2, 16, 256, 512], P(None, 'dp', 'blk')
- grad_mask_token: float32 [512], replicated
- grad_norm1_gain: float32 [512], replicated
- grad_norm1_bias: float32 [512], replicated
- grad_w_qkv: float32 [512, 1536], replicated
- grad_b_query: float32 [512], replicated
- grad_b_value: float32 [512], replicated
- grad_w_out: float32 [512, 512], replicated
- grad_b_out: float32 [512], replicated
- grad_norm2_gain: float32 [512], replicated
- grad_norm2_bias: float32 [512], replicated
- grad_w_up: float32 [512, 2048], replicated
- grad_b_up: float32 [2048], replicated
- grad_w_down: float32 [2048, 512], replicated
- grad_b_down: float32 [512], replicated
The draws below stay inside these ranges and needn't reach their ends.
Inputs may be any that keep to these rules, and one draw needn't show every extreme that they name: `buckets`: all images that one index of dp holds in one micro-batch share this bucket: 0, 1, 2 stand for 100, 196, 256 patches; every image's patches are split evenly over the 4 devices of blk, each device's share in the first rows of its 64 slots, the rest padding.
All inputs are finite; a program needn't handle non-finite values. No bound on the sum of `mask_flags` on one device may be relied on, other than what follows from the above.
Results may differ from the reference program's by a relative error of at most 0.02.
Values may be sent and summed in bfloat16 or wider, within the bound.
No kernel may reach another device: no remote copies, remote signals or barrier semaphores. Data moves between devices by JAX's collectives and lax.ppermute only.
A program may use at most 128 MiB of HBM per device.

```python
import math
import jax
import jax.numpy as jnp
from jax import lax

D = 512
HEADS = 16
FF = 2048
SLOT = 256
MB = 2
NIMG = 16
N_DP = 8
N_BLK = 4


def set_ends(values, own_key, low, largest):
    place = [jax.random.randint(jax.random.fold_in(own_key, axis), (), 0, length) for axis, length in enumerate(values.shape)]
    main_axis = values.shape.index(max(values.shape))
    beside = place[:main_axis] + [(place[main_axis] + 1) % values.shape[main_axis]] + place[main_axis + 1:]
    return values.at[tuple(place)].set(low).at[tuple(beside)].set(largest)


def shard_levels(stream_key, extent, cuts, smallest, top_value):
    loudness = 1.0
    for dim, shards_of in cuts:
        draws = jax.random.uniform(jax.random.fold_in(jax.random.fold_in(stream_key, 6), dim), (shards_of,), jnp.float32, smallest / len(cuts), top_value / len(cuts))
        loudness = loudness * jnp.repeat(jnp.exp(draws), extent[dim] // shards_of).reshape((-1,) + (1,) * (len(extent) - 1 - dim))
    return loudness


def normal_values(stream_key, extent, deviation, limit, cuts=(), kind=jnp.bfloat16):
    entries = deviation * jax.random.normal(stream_key, extent, jnp.float32)
    if cuts:
        entries = entries * shard_levels(stream_key, extent, cuts, -0.22, 0.18)
    return jnp.clip(entries, -limit, limit).astype(kind)


def setup_inputs(seed: int = 0) -> dict:
    keys = jax.random.split(jax.random.key(seed), 19)
    tokens = normal_values(keys[0], (MB, NIMG, SLOT, D), 1.0, 6.0, ((1, 8), (2, 4)))
    mask_flags = set_ends((jax.random.randint(keys[1], (MB, NIMG, SLOT), 0, 4) < 3).astype(jnp.int32), jax.random.fold_in(keys[1], 1), 0, 1)
    buckets = set_ends(jax.random.randint(keys[2], (MB, N_DP), 0, 3), jax.random.fold_in(keys[2], 1), 0, 2).astype(jnp.int32)
    cotangent = normal_values(keys[3], (MB, NIMG, SLOT, D), 1.0, 6.0, ((1, 8), (2, 4)))
    mask_token = normal_values(keys[4], (D,), 1.0, 5.0)
    norm1_gain = jnp.clip(1.0 + 0.1 * jax.random.normal(keys[5], (D,), jnp.float32), 0.5, 1.5).astype(jnp.bfloat16)
    norm1_bias = normal_values(keys[6], (D,), 0.3, 1.5)
    w_qkv = normal_values(keys[7], (D, 3 * D), D ** -0.5, 0.25)
    b_query = normal_values(keys[8], (D,), 0.3, 1.5)
    b_value = normal_values(keys[9], (D,), 0.3, 1.5)
    w_out = normal_values(keys[10], (D, D), (D // 16) ** -0.5, 1.0)
    b_out = normal_values(keys[11], (D,), 0.3, 1.5)
    norm2_gain = jnp.clip(1.0 + 0.1 * jax.random.normal(keys[12], (D,), jnp.float32), 0.5, 1.5).astype(jnp.bfloat16)
    norm2_bias = normal_values(keys[13], (D,), 0.3, 1.5)
    w_up = normal_values(keys[14], (D, FF), D ** -0.5, 0.25)
    b_up = normal_values(keys[15], (FF,), 0.3, 1.5)
    w_down = normal_values(keys[16], (FF, D), FF ** -0.5, 0.125)
    b_down = normal_values(keys[17], (D,), 0.3, 1.5)
    return dict(tokens=tokens, mask_flags=mask_flags, buckets=buckets, cotangent=cotangent, mask_token=mask_token, norm1_gain=norm1_gain, norm1_bias=norm1_bias, w_qkv=w_qkv, b_query=b_query, b_value=b_value, w_out=w_out, b_out=b_out, norm2_gain=norm2_gain, norm2_bias=norm2_bias, w_up=w_up, b_up=b_up, w_down=w_down, b_down=b_down)


@jax.custom_vjp
def low(v):
    return lax.optimization_barrier(v.astype(jnp.bfloat16)).astype(jnp.float32)

@jax.custom_vjp
def low_back(v):
    return v

def low_keep(v):
    return (low(v), None)

def low_pass(kept, grad):
    return (grad,)

def back_keep(v):
    return (v, None)

def back_low(kept, grad):
    return (low(grad),)
low.defvjp(low_keep, low_pass)
low_back.defvjp(back_keep, back_low)

def layer_norm(inputs, norm_gain, norm_shift):
    centre = lax.optimization_barrier(jnp.mean(inputs, axis=-1, keepdims=True))
    centred = inputs - centre
    spread = lax.optimization_barrier(jnp.mean(centred * centred, axis=-1, keepdims=True))
    return centred * lax.rsqrt(spread + 1e-06) * norm_gain + norm_shift

def exact_dot(lhs_rows, rhs_cols):
    return jnp.dot(lhs_rows, rhs_cols, precision=lax.Precision.HIGHEST, preferred_element_type=jnp.float32)

def block_forward(params, tok_block, flag_block, valid_block):
    mask_vec, gain_one, shift_one, w_proj, bias_query, bias_value, w_after, bias_after, gain_two, shift_two, w_expand, bias_expand, w_reduce, bias_reduce = params
    images, slots, width = tok_block.shape
    head_size = width // HEADS
    filled = jnp.where(flag_block[..., None] == 1, mask_vec, tok_block)
    flat_rows = filled.reshape(images * slots, width)
    normed_one = low(layer_norm(flat_rows, gain_one, shift_one))
    qkv_bias = jnp.concatenate([bias_query, jnp.zeros_like(bias_query), bias_value])
    projected = low_back(low(exact_dot(normed_one, w_proj) + qkv_bias))
    queries = projected[:, :width].reshape(images, slots, HEADS, head_size)
    key_rows = projected[:, width:2 * width].reshape(images, slots, HEADS, head_size)
    value_rows = projected[:, 2 * width:].reshape(images, slots, HEADS, head_size)
    scores = jnp.einsum('iqhd,ikhd->ihqk', queries, key_rows, precision=lax.Precision.HIGHEST) * head_size ** (-0.5)
    scores = low_back(scores)
    scores = jnp.where(valid_block[:, None, None, :], scores, -1e+30)
    weights = low(jax.nn.softmax(scores, axis=-1))
    attended = jnp.einsum('ihqk,ikhd->iqhd', weights, value_rows, precision=lax.Precision.HIGHEST)
    attended = low_back(low(attended.reshape(images * slots, width)))
    attn_out = low_back(exact_dot(attended, w_after) + bias_after)
    middle = flat_rows + attn_out
    normed_two = low(layer_norm(middle, gain_two, shift_two))
    hidden = low_back(exact_dot(normed_two, w_expand) + bias_expand)
    activated = low(jax.nn.gelu(hidden, approximate=False))
    branch = low_back(exact_dot(activated, w_reduce) + bias_reduce)
    return (middle + branch).reshape(images, slots, width)

def reference(tokens, mask_flags, buckets, cotangent, mask_token, norm1_gain, norm1_bias, w_qkv, b_query, b_value, w_out, b_out, norm2_gain, norm2_bias, w_up, b_up, w_down, b_down):
    params = tuple((item.astype(jnp.float32) for item in (mask_token, norm1_gain, norm1_bias, w_qkv, b_query, b_value, w_out, b_out, norm2_gain, norm2_bias, w_up, b_up, w_down, b_down)))
    micro_count, image_count, slot_count, width = tokens.shape
    share = slot_count // N_BLK
    per_device = image_count // N_DP
    row_quota = jnp.array([25, 49, 64], jnp.int32)[buckets]
    row_quota = jnp.repeat(row_quota, per_device, axis=1)
    places = jnp.arange(slot_count, dtype=jnp.int32) % share
    valid_rows = places[None, None, :] < row_quota[:, :, None]
    group_size = math.gcd(image_count, 16)
    blocks = micro_count * image_count // group_size

    def regroup(stacked):
        return stacked.reshape((blocks, group_size) + stacked.shape[2:])

    def one_block(totals, items):
        tok_block, flag_block, valid_block, cot_block = items

        def forward(param_set, tok_values):
            return block_forward(param_set, tok_values, flag_block, valid_block)
        outputs, backward = jax.vjp(forward, params, tok_block.astype(jnp.float32))
        weight_grads, token_grads = backward(cot_block.astype(jnp.float32) * valid_block[..., None].astype(jnp.float32))
        totals = jax.tree.map(jnp.add, totals, weight_grads)
        return (totals, (outputs.astype(jnp.bfloat16), token_grads))
    zero_sums = tuple((jnp.zeros_like(item) for item in params))
    totals, (outputs, token_grads) = lax.scan(one_block, zero_sums, (regroup(tokens), regroup(mask_flags), regroup(valid_rows), regroup(cotangent)))
    image_total = float(micro_count * image_count)
    grad_mask, grad_gain_one, grad_shift_one, grad_proj, grad_bias_query, grad_bias_value, grad_after, grad_bias_after, grad_gain_two, grad_shift_two, grad_expand, grad_bias_expand, grad_reduce, grad_bias_reduce = tuple((item / image_total for item in totals))
    block_out = outputs.reshape(tokens.shape)
    token_grad = token_grads.reshape(tokens.shape)
    return (block_out, token_grad, grad_mask, grad_gain_one, grad_shift_one, grad_proj, grad_bias_query, grad_bias_value, grad_after, grad_bias_after, grad_gain_two, grad_shift_two, grad_expand, grad_bias_expand, grad_reduce, grad_bias_reduce)
```

```python
import functools

import jax
import jax.numpy as jnp
from jax import lax
from jax.experimental import pallas as pl
from jax.experimental.pallas import tpu as pltpu
from jax.sharding import PartitionSpec as P

HEADS = 16
LANES = 128
EPS = 1e-06
LOG2E = 1.4426950408889634
BF16 = jnp.bfloat16
F32 = jnp.float32
VMEM_LIMIT = 44 * 1024 * 1024


def dot(a, b):
    return jnp.dot(a, b, preferred_element_type=F32)


def dot_nt(a, b):
    return lax.dot_general(a, b, (((1,), (1,)), ((), ())), preferred_element_type=F32)


def dot_tn(a, b):
    return lax.dot_general(a, b, (((0,), (0,)), ((), ())), preferred_element_type=F32)


def norm_stats(rows):
    centre = jnp.mean(rows, axis=-1, keepdims=True)
    centred = rows - centre
    spread = jnp.mean(centred * centred, axis=-1, keepdims=True)
    rstd = lax.rsqrt(spread + EPS)
    return centred * rstd, rstd


def norm_back(grad_normed, xhat, rstd, gain):
    grad_xhat = grad_normed * gain
    first = jnp.mean(grad_xhat, axis=-1, keepdims=True)
    second = jnp.mean(grad_xhat * xhat, axis=-1, keepdims=True)
    return rstd * (grad_xhat - first - xhat * second)


class Pieces:
    def __init__(self, rows, cols, chips):
        self.rows = rows
        self.half = cols // 2
        self.row_blocks = min(chips, rows // 16)
        self.lane_blocks = chips // self.row_blocks
        self.height = rows // self.row_blocks
        self.width = self.half // self.lane_blocks
        self.tall = self.height * self.width // LANES


def relative(core, x, y, z, ax, ay, az, depth):
    px, py = ax ^ x, ay ^ y
    return jnp.where(core == 0, px * 2 + py, py * 2 + px) * depth + (az ^ z)


def chip_of(index, depth):
    return index // (2 * depth), (index // depth) % 2, index % depth


def absolute(core, x, y, z, index, depth):
    first, second, az = chip_of(index, depth)
    ax = jnp.where(core == 0, first ^ x, second ^ x)
    ay = jnp.where(core == 0, second ^ y, first ^ y)
    return (ax * 2 + ay) * depth + (az ^ z)


def store_pieces(out_ref, core, place, depth, pieces, base, value, row_start):
    x, y, z = place
    for first in range(0, value.shape[0], pieces.height):
        row_block = (row_start + first) // pieces.height
        for lane_block in range(pieces.lane_blocks):
            index = row_block * pieces.lane_blocks + lane_block
            rel = relative(core, x, y, z, *chip_of(index, depth), depth)
            for j in range(pieces.width // LANES):
                at = base + j * pieces.height
                lane = lane_block * pieces.width + j * LANES
                out_ref[rel, at : at + pieces.height, :] = value[
                    first : first + pieces.height, lane : lane + LANES
                ].astype(BF16)


def weight_grad(keep_ref, send_ref, core, place, depth, pieces, base, lhs, rhs_ref):
    stripe = max(pieces.height, min(512, pieces.rows))
    for out_ref, owner in ((send_ref, core ^ 1), (keep_ref, core)):
        rhs = rhs_ref[:, pl.ds(pl.multiple_of(owner * pieces.half, LANES), pieces.half)]
        for start in range(0, pieces.rows, stripe):
            value = dot_tn(lhs[:, start : start + stripe], rhs)
            store_pieces(out_ref, owner, place, depth, pieces, base, value, start)


def place_of(meta):
    return meta[0], (meta[1], meta[2], meta[3])


def fill_kernel(meta, tokens, flags, mask_token, *outs):
    blk = meta[5]
    count, share, _ = tokens.shape
    eye = lax.broadcasted_iota(jnp.int32, (share, share), 0) == lax.broadcasted_iota(
        jnp.int32, (share, share), 1
    )
    for k in range(count):
        at = blk ^ k
        flag = flags[pl.ds(at, 1), 0, :]
        column = jnp.sum(jnp.where(eye, flag, 0), axis=1, keepdims=True)
        outs[k][...] = jnp.where(
            column == 1, mask_token[...].astype(F32), tokens[at].astype(F32)
        ).astype(BF16)


def cotangent_kernel(meta, cotangent, flags, *outs):
    blk = meta[5]
    count, share, _ = cotangent.shape
    for k in range(count):
        at = blk ^ k
        outs[k][:share, :] = cotangent[at]
        outs[k][share:, :] = jnp.zeros((16, outs[k].shape[1]), BF16)
        row = lax.broadcasted_iota(jnp.int32, (16, share), 0) == 0
        flag = (flags[pl.ds(at, 1), 0, :] == 1).astype(F32)
        outs[k][share:, :share] = jnp.where(row, flag, 0.0).astype(BF16)


def forward_kernel(
    depth,
    down,
    count,
    share,
    meta,
    *refs,
):
    refs = list(refs)
    xs = [refs.pop(0) for _ in range(count)]
    cs = [refs.pop(0) for _ in range(count)]
    (
        gain1, bias1, w_qkv, b_query, b_value, w_out, b_out, gain2, bias2, w_up, b_up,
        qkv_ref, p_ref, rinv_ref, o_ref, x2_ref, n2_ref, h_ref, gp_ref, g_ref, keep_ref, send_ref,
    ) = refs
    core, place = place_of(meta)
    quota = meta[4]
    width = xs[0].shape[1]
    head = width // HEADS
    rows = count * share
    live_rows = lax.broadcasted_iota(jnp.int32, (share, 1), 0) < quota
    for k in range(count):
        g_ref[k * share : (k + 1) * share, :] = jnp.where(
            live_rows, cs[k][:share, :].astype(F32), 0.0
        ).astype(BF16)
    x = jnp.concatenate([ref[...] for ref in xs], axis=0).astype(F32)
    xhat, _ = norm_stats(x)
    n1 = (xhat * gain1[...].astype(F32) + bias1[...].astype(F32)).astype(BF16)
    for part in range(3):
        cols = slice(part * width, (part + 1) * width)
        value = dot(n1, w_qkv[:, cols])
        if part == 0:
            value = value + b_query[...].astype(F32)
        if part == 2:
            value = value + b_value[...].astype(F32)
        qkv_ref[:, cols] = value.astype(BF16)
    key = lax.broadcasted_iota(jnp.int32, (1, rows), 1)
    mask_row = jnp.where(key % share < quota, 0.0, -1e30).astype(F32)
    lane_head = lax.broadcasted_iota(jnp.int32, (1, LANES), 1) // head
    scale = head ** (-0.5) * LOG2E
    per = LANES // head
    ones = jnp.ones((rows, LANES), BF16)
    for group in range(width // LANES):
        at = group * LANES
        q = qkv_ref[:, at : at + LANES]
        keys = qkv_ref[:, width + at : width + at + LANES]
        values = jnp.concatenate(
            [qkv_ref[:, 2 * width + at : 2 * width + at + LANES], ones], axis=1
        )
        acc = jnp.zeros((rows, LANES), F32)
        racc = jnp.zeros((rows, LANES), F32)
        for i in range(per):
            here = lane_head == i
            qm = q * here.astype(F32).astype(BF16)
            s = dot_nt(qm, keys) * scale + mask_row
            top = jnp.max(s, axis=1, keepdims=True)
            p = jnp.exp2(s - top).astype(BF16)
            p_ref[group * per + i] = p
            both = dot(p, values)
            rinv = 1.0 / both[:, LANES:]
            acc = jnp.where(here, both[:, :LANES] * rinv, acc)
            racc = jnp.where(here, rinv, racc)
        o_ref[:, at : at + LANES] = acc.astype(BF16)
        rinv_ref[:, at : at + LANES] = racc
    x2 = x + (dot(o_ref[...], w_out[...]) + b_out[...].astype(F32))
    x2_ref[...] = x2
    xhat2, _ = norm_stats(x2)
    n2 = (xhat2 * gain2[...].astype(F32) + bias2[...].astype(F32)).astype(BF16)
    n2_ref[...] = n2
    hidden = w_up.shape[1]
    step = 512
    for start in range(0, hidden, step):
        cols = slice(start, start + step)
        u = dot(n2, w_up[:, cols]) + b_up[:, cols].astype(F32)
        cdf = 0.5 + 0.5 * lax.erf(u * (0.5**0.5))
        pdf = jnp.exp(-0.5 * u * u) * 0.3989422804014327
        h_ref[:, cols] = (u * cdf).astype(BF16)
        gp_ref[:, cols] = (cdf + u * pdf).astype(BF16)
    weight_grad(keep_ref, send_ref, core, place, depth, down, 0, h_ref, g_ref)


def middle_kernel(
    depth,
    up,
    after,
    meta,
    g_ref, gp_ref, h_ref, n2_ref, o_ref, x2_ref, gain2, w_up, w_down, b_down,
    keep_ref, send_ref, dx2_ref, dx2r_ref, out_ref, small_ref, du_ref,
):
    core, place = place_of(meta)
    g = g_ref[...]
    hidden = w_up.shape[1]
    width = g.shape[1]
    step = 512
    small_ref[...] = jnp.zeros(small_ref.shape, F32)
    dn2 = jnp.zeros((g.shape[0], width), F32)
    for start in range(0, hidden, step):
        cols = slice(start, start + step)
        dh = dot_nt(g, w_down[cols, :])
        du = (dh * gp_ref[:, cols].astype(F32)).astype(BF16)
        du_ref[:, cols] = du
        small_ref[0:1, cols] = jnp.sum(du.astype(F32), axis=0, keepdims=True)
        dn2 = dn2 + dot_nt(du, w_up[:, cols])
    x2 = x2_ref[...]
    xhat, rstd = norm_stats(x2)
    gf = g.astype(F32)
    dx2 = gf + norm_back(dn2, xhat, rstd, gain2[...].astype(F32))
    dx2_ref[...] = dx2
    dx2r = dx2.astype(BF16)
    dx2r_ref[...] = dx2r
    small_ref[1:2, 0:width] = jnp.sum(dx2r.astype(F32), axis=0, keepdims=True)
    small_ref[1:2, width : 2 * width] = jnp.sum(dn2 * xhat, axis=0, keepdims=True)
    small_ref[1:2, 2 * width : 3 * width] = jnp.sum(dn2, axis=0, keepdims=True)
    small_ref[1:2, 3 * width : 4 * width] = jnp.sum(gf, axis=0, keepdims=True)
    weight_grad(keep_ref, send_ref, core, place, depth, up, 0, n2_ref, du_ref)
    weight_grad(keep_ref, send_ref, core, place, depth, after, up.tall, o_ref, dx2r_ref)
    out_ref[...] = (x2 + (dot(h_ref[...], w_down[...]) + b_down[...].astype(F32))).astype(BF16)


def backward_kernel(
    depth,
    proj,
    count,
    share,
    meta,
    *refs,
):
    refs = list(refs)
    xs = [refs.pop(0) for _ in range(count)]
    cs = [refs.pop(0) for _ in range(count)]
    qkv_ref, p_ref, rinv_ref, o_ref, dx2_ref, dx2r_ref, block_ref, sub_ref, gain1, bias1, w_qkv, w_out = refs[:12]
    refs = refs[12:]
    results = [refs.pop(0) for _ in range(count)]
    keep_ref, send_ref, dqkv_ref, small = refs
    core, place = place_of(meta)
    rows = count * share
    width = xs[0].shape[1]
    head = width // HEADS
    per = LANES // head
    d_o = dot_nt(dx2r_ref[...], w_out[...]).astype(BF16).astype(F32)
    d_scaled = d_o * rinv_ref[...]
    product = (d_scaled * o_ref[...].astype(F32)).astype(BF16)
    d_scaled = d_scaled.astype(BF16)
    lane_head = lax.broadcasted_iota(jnp.int32, (1, LANES), 1) // head
    minus = jnp.full((rows, LANES), -1.0, BF16)
    scale = head ** (-0.5)
    for group in range(width // LANES):
        at = group * LANES
        q = qkv_ref[:, at : at + LANES]
        keys = qkv_ref[:, width + at : width + at + LANES]
        values = jnp.concatenate(
            [qkv_ref[:, 2 * width + at : 2 * width + at + LANES], minus], axis=1
        )
        ds_o = d_scaled[:, at : at + LANES]
        pr_o = product[:, at : at + LANES]
        dq = jnp.zeros((rows, LANES), F32)
        dk = jnp.zeros((rows, LANES), F32)
        dv = jnp.zeros((rows, LANES), F32)
        for i in range(per):
            here = lane_head == i
            mask = here.astype(F32).astype(BF16)
            lhs = jnp.concatenate([ds_o * mask, pr_o * mask], axis=1)
            p = p_ref[group * per + i]
            ds = (p.astype(F32) * dot_nt(lhs, values)).astype(BF16)
            dq = jnp.where(here, dot(ds, keys), dq)
            dk = jnp.where(here, dot_tn(ds, q), dk)
            dv = jnp.where(here, dot_tn(p, ds_o), dv)
        dqkv_ref[:, at : at + LANES] = (dq * scale).astype(BF16)
        dqkv_ref[:, width + at : width + at + LANES] = (dk * scale).astype(BF16)
        dqkv_ref[:, 2 * width + at : 2 * width + at + LANES] = dv.astype(BF16)
    x = jnp.concatenate([ref[...] for ref in xs], axis=0).astype(F32)
    xhat, rstd = norm_stats(x)
    gain = gain1[...].astype(F32)
    n1 = (xhat * gain + bias1[...].astype(F32)).astype(BF16)
    weight_grad(keep_ref, send_ref, core, place, depth, proj, 0, n1, dqkv_ref)
    dn1 = dot_nt(dqkv_ref[...], w_qkv[...])
    dx = (dx2_ref[...] + norm_back(dn1, xhat, rstd, gain)).astype(BF16)
    d_mask = jnp.zeros((16, width), F32)
    for k in range(count):
        part = dx[k * share : (k + 1) * share, :]
        d_mask = d_mask + dot(cs[k][share : share + 16, :share], part)
        results[k][:share, :] = block_ref[k * share : (k + 1) * share, :]
        results[k][share:, :] = part
    blocks = small.shape[0]
    small[...] = jnp.zeros(small.shape, F32)
    wide = [
        d_mask[0:1, :],
        jnp.sum(dn1 * xhat, axis=0, keepdims=True),
        jnp.sum(dn1, axis=0, keepdims=True),
        jnp.sum(dqkv_ref[:, :width].astype(F32), axis=0, keepdims=True),
        jnp.sum(dqkv_ref[:, 2 * width :].astype(F32), axis=0, keepdims=True),
        sub_ref[1:2, :],
        sub_ref[0:1, :],
    ]
    lines = [v[:, j : j + LANES] for v in wide for j in range(0, v.shape[1], LANES)]
    each = -(-len(lines) // blocks)
    for i, line in enumerate(lines):
        small[i // each, i % each : i % each + 1, :] = line
    chips = blocks // 2
    x0, y0, z0 = place
    for out_ref, owner in ((send_ref, core ^ 1), (keep_ref, core)):
        for index in range(chips):
            rel = relative(owner, x0, y0, z0, *chip_of(index, depth), depth)
            out_ref[rel, proj.tall : proj.tall + 16, :] = small[owner * chips + index].astype(BF16)


def load_pieces(refs, rel):
    for ref in refs:
        if rel < ref.shape[0]:
            return ref, rel
        rel -= ref.shape[0]


def gather_kernel(depth, layout, scale, small_at, sizes, meta, *refs):
    own, other = refs[:3], refs[3:6]
    outs = refs[6 : 6 + len(layout)]
    rest = refs[6 + len(layout) :]
    core, (x, y, z) = place_of(meta)
    chips = sum(ref.shape[0] for ref in own)
    for held, owner in ((own, core), (other, core ^ 1)):
        for rel in range(chips):
            ref, at_block = load_pieces(held, rel)
            index = absolute(owner, x, y, z, rel, depth)
            for out, (pieces, base) in zip(outs, layout):
                row = pl.multiple_of((index // pieces.lane_blocks) * pieces.height, 8)
                lane = owner * pieces.half + (index % pieces.lane_blocks) * pieces.width
                for j in range(pieces.width // LANES):
                    at = base + j * pieces.height
                    block = ref[at_block, at : at + pieces.height, :]
                    out[
                        pl.ds(row, pieces.height),
                        pl.ds(pl.multiple_of(lane + j * LANES, LANES), LANES),
                    ] = block.astype(F32) * scale
            if rest:
                small = rest[-1]
                small[owner * chips + index] = (
                    ref[at_block, small_at : small_at + 16, :].astype(F32) * scale
                )
    if rest:
        small = rest[-1]
        lines = sum(sizes) // LANES
        each = -(-lines // (2 * chips))
        line = 0
        for out, size in zip(rest[:-1], sizes):
            for j in range(size // LANES):
                out[:, j * LANES : (j + 1) * LANES] = small[
                    line // each, line % each : line % each + 1, :
                ]
                line += 1


def finish_kernel(meta, flags, *refs):
    count = len(refs) - 2
    block_out, token_grad = refs[-2:]
    share = block_out.shape[1]
    blk = meta[5]
    eye = lax.broadcasted_iota(jnp.int32, (share, share), 0) == lax.broadcasted_iota(
        jnp.int32, (share, share), 1
    )
    for k in range(count):
        at = blk ^ k
        block_out[at] = refs[k][:share, :]
        flag = flags[pl.ds(at, 1), 0, :]
        column = jnp.sum(jnp.where(eye, flag, 0), axis=1, keepdims=True)
        token_grad[at] = jnp.where(column == 1, 0.0, refs[k][share:, :].astype(F32))


SCALARS = pl.BlockSpec(memory_space=pltpu.SMEM)
WHOLE = pl.BlockSpec(memory_space=pltpu.VMEM)


def call(kernel, outs, *args, scratch=(), flops=0, name=None):
    size = sum(a.size * a.dtype.itemsize for a in args) + sum(
        o.size * o.dtype.itemsize for o in outs
    )
    return pl.pallas_call(
        kernel,
        out_shape=tuple(outs),
        in_specs=[SCALARS] + [WHOLE] * (len(args) - 1),
        out_specs=tuple([WHOLE] * len(outs)),
        scratch_shapes=list(scratch),
        compiler_params=pltpu.CompilerParams(vmem_limit_bytes=VMEM_LIMIT),
        cost_estimate=pl.CostEstimate(flops=flops, bytes_accessed=size, transcendentals=0),
        name=name,
    )(*args)


def shape(dims, kind=BF16):
    return jax.ShapeDtypeStruct(tuple(dims), kind)


def add(*parts):
    total = parts[0].astype(F32)
    for part in parts[1:]:
        total = total + part.astype(F32)
    return total.astype(BF16)


def shards(
    dp_size,
    blk_size,
    tokens,
    mask_flags,
    buckets,
    cotangent,
    mask_token,
    norm1_gain,
    norm1_bias,
    w_qkv,
    b_query,
    b_value,
    w_out,
    b_out,
    norm2_gain,
    norm2_bias,
    w_up,
    b_up,
    w_down,
    b_down,
):
    micro_count, images, share, width = tokens.shape
    hidden = w_up.shape[1]
    count = micro_count * images
    rows = count * share
    depth = dp_size // 2
    chips = 4 * depth
    total_images = float(micro_count * images * dp_size)

    dp = lax.axis_index("dp")
    blk = lax.axis_index("blk")
    bucket = buckets[blk // images, 0]
    quota = jnp.where(bucket == 0, 25, jnp.where(bucket == 1, 49, 64))
    meta = jnp.stack([blk % 2, blk // 2, dp % 2, dp // 2, quota, blk]).astype(jnp.int32)

    def pairs(change):
        out = []
        for d in range(dp_size):
            for b in range(blk_size):
                nz, ny, nx, nc = change(d // 2, d % 2, b // 2, b % 2)
                out.append((d * blk_size + b, (nz * 2 + ny) * blk_size + nx * 2 + nc))
        return out

    def send(value, change):
        return lax.ppermute(value, ("dp", "blk"), pairs(change))

    def core_pair(z, y, x, c):
        return z, y, x, c ^ 1

    def first_pair(z, y, x, c):
        return (z, y, x ^ 1, c) if c == 0 else (z, y ^ 1, x, c)

    def second_pair(z, y, x, c):
        return (z, y ^ 1, x, c) if c == 0 else (z, y, x ^ 1, c)

    def depth_pair(k):
        return lambda z, y, x, c: (z ^ k, y, x, c)

    def image_pair(k):
        return lambda z, y, x, c: (z, y, x ^ (k >> 1), c ^ (k & 1))

    def reduce_blocks(keep, sent):
        got = send(sent, core_pair)
        h = chips // 2
        away = add(keep[h:], got[h:])
        stay = add(keep[:h], got[:h])
        got = send(away, first_pair)
        h = chips // 4
        away = add(stay[h:], got[h:])
        stay = add(stay[:h], got[:h])
        got = send(away, second_pair)
        held = add(stay, got)
        return add(held[0], *[send(held[k], depth_pair(k)) for k in range(1, depth)])

    def gather_blocks(block):
        first = jnp.stack([block] + [send(block, depth_pair(k)) for k in range(1, depth)])
        second = send(first, second_pair)
        third = send(jnp.concatenate([first, second]), first_pair)
        mine = (first, second, third)
        return mine + tuple(send(a, core_pair) for a in mine)

    def wide(v):
        return v.reshape(1, -1)

    flags = mask_flags.reshape(count, 1, share)
    xs = call(
        fill_kernel,
        [shape((share, width))] * count,
        meta,
        tokens.reshape(count, share, width),
        flags,
        wide(mask_token),
        name="fill",
    )
    xs = [xs[0]] + [send(xs[k], image_pair(k)) for k in range(1, count)]
    cs = call(
        cotangent_kernel,
        [shape((share + 16, width))] * count,
        meta,
        cotangent.reshape(count, share, width),
        flags,
        name="cotangents",
    )
    cs = [cs[0]] + [send(cs[k], image_pair(k)) for k in range(1, count)]

    down = Pieces(hidden, width, chips)
    up = Pieces(width, hidden, chips)
    after = Pieces(width, width, chips)
    proj = Pieces(width, 3 * width, chips)

    qkv, p, rinv, o, x2, n2, h, gp, g, keep1, send1 = call(
        functools.partial(forward_kernel, depth, down, count, share),
        [
            shape((rows, 3 * width)),
            shape((HEADS, rows, rows)),
            shape((rows, width), F32),
            shape((rows, width)),
            shape((rows, width), F32),
            shape((rows, width)),
            shape((rows, hidden)),
            shape((rows, hidden)),
            shape((rows, width)),
            shape((chips, down.tall, LANES)),
            shape((chips, down.tall, LANES)),
        ],
        meta,
        *xs,
        *cs,
        wide(norm1_gain),
        wide(norm1_bias),
        w_qkv,
        wide(b_query),
        wide(b_value),
        w_out,
        wide(b_out),
        wide(norm2_gain),
        wide(norm2_bias),
        w_up,
        wide(b_up),
        flops=2 * rows * width * (3 * width + width + 2 * hidden),
        name="forward",
    )
    keep2, send2, dx2, dx2r, block, sub = call(
        functools.partial(middle_kernel, depth, up, after),
        [
            shape((chips, up.tall + after.tall, LANES)),
            shape((chips, up.tall + after.tall, LANES)),
            shape((rows, width), F32),
            shape((rows, width)),
            shape((rows, width)),
            shape((8, hidden), F32),
        ],
        meta,
        g,
        gp,
        h,
        n2,
        o,
        x2,
        wide(norm2_gain),
        w_up,
        w_down,
        wide(b_down),
        scratch=[pltpu.VMEM((rows, hidden), BF16)],
        flops=2 * rows * width * (4 * hidden + width),
        name="middle",
    )
    *results, keep3, send3 = call(
        functools.partial(backward_kernel, depth, proj, count, share),
        [shape((2 * share, width))] * count + [shape((chips, proj.tall + 16, LANES))] * 2,
        meta,
        *xs,
        *cs,
        qkv,
        p,
        rinv,
        o,
        dx2,
        dx2r,
        block,
        sub,
        wide(norm1_gain),
        wide(norm1_bias),
        w_qkv,
        w_out,
        scratch=[
            pltpu.VMEM((rows, 3 * width), BF16),
            pltpu.VMEM((2 * chips, 16, LANES), F32),
        ],
        flops=2 * rows * width * (7 * width),
        name="backward",
    )

    done1 = gather_blocks(reduce_blocks(keep1, send1))
    done2 = gather_blocks(reduce_blocks(keep2, send2))
    done3 = gather_blocks(reduce_blocks(keep3, send3))

    def whole(done, layout, small_at=0, sizes=(), name=None):
        outs = [shape((p.rows, 2 * p.half), F32) for p, _ in layout]
        scratch = []
        if sizes:
            outs += [shape((1, n), F32) for n in sizes]
            scratch = [pltpu.VMEM((2 * chips, 16, LANES), F32)]
        return call(
            functools.partial(
                gather_kernel, depth, layout, 1.0 / total_images, small_at, sizes
            ),
            outs,
            meta,
            *done,
            scratch=scratch,
            name=name,
        )

    (grad_down,) = whole(done1, [(down, 0)], name="gather_down")
    grad_up, grad_out = whole(done2, [(up, 0), (after, up.tall)], name="gather_up")
    sizes = (width,) * 9 + (hidden,)
    grad_proj, *small = whole(done3, [(proj, 0)], proj.tall, sizes, name="gather_proj")
    mask_g, gain1_g, bias1_g, query_g, value_g, after_g, gain2_g, bias2_g, reduce_g, expand_g = [
        v.reshape(-1) for v in small
    ]

    results = [results[0]] + [send(results[k], image_pair(k)) for k in range(1, count)]
    block_out, token_grad = call(
        finish_kernel,
        [shape((count, share, width)), shape((count, share, width), F32)],
        meta,
        flags,
        *results,
        name="finish",
    )
    return (
        block_out.reshape(tokens.shape),
        token_grad.reshape(tokens.shape),
        mask_g,
        gain1_g,
        bias1_g,
        grad_proj,
        query_g,
        value_g,
        grad_out,
        after_g,
        gain2_g,
        bias2_g,
        grad_up,
        expand_g,
        grad_down,
        reduce_g,
    )


def solution(mesh):
    rows = P(None, "dp", "blk", None)
    placed = (rows, P(None, "dp", "blk"), P(None, "dp"), rows) + (P(),) * 14
    return jax.shard_map(
        functools.partial(shards, mesh.shape["dp"], mesh.shape["blk"]),
        mesh=mesh,
        in_specs=placed,
        out_specs=(rows, rows) + (P(),) * 14,
        check_vma=False,
    )
```

```python
import functools

import jax
import jax.numpy as jnp
from jax import lax
from jax.experimental import pallas as pl
from jax.experimental.pallas import tpu as pltpu
from jax.sharding import PartitionSpec as P

HEADS = 16
LANES = 128
EPS = 1e-06
LOG2E = 1.4426950408889634
BF16 = jnp.bfloat16
F32 = jnp.float32
ORDERS = (('zxy', 'zyx'), ('yxz', 'xyz'), ('xyz', 'yxz'))
TIES = (((0, 1), (3, 0)), ((1, 0), (3, 0)), ((1, 4), (5, 0)))
RESULTS = (3, 0)
WRITTEN = ()
US = {'forward': 15}
VMEM_LIMIT = 24 * 1024 * 1024


def dot(a, b):
    return jnp.dot(a, b, preferred_element_type=F32)


def dot_nt(a, b):
    return lax.dot_general(a, b, (((1,), (1,)), ((), ())), preferred_element_type=F32)


def dot_tn(a, b):
    return lax.dot_general(a, b, (((0,), (0,)), ((), ())), preferred_element_type=F32)


def row(ref):
    return ref[...].astype(F32).reshape(1, -1)


def norm_stats(rows):
    centre = jnp.mean(rows, axis=-1, keepdims=True)
    centred = rows - centre
    spread = jnp.mean(centred * centred, axis=-1, keepdims=True)
    rstd = lax.rsqrt(spread + EPS)
    return centred * rstd, rstd


def norm_back(grad_normed, xhat, rstd, gain):
    grad_xhat = grad_normed * gain
    first = jnp.mean(grad_xhat, axis=-1, keepdims=True)
    second = jnp.mean(grad_xhat * xhat, axis=-1, keepdims=True)
    return rstd * (grad_xhat - first - xhat * second)


class Pieces:
    def __init__(self, rows, cols, chips):
        self.rows = rows
        self.half = cols // 2
        self.row_blocks = min(chips, rows // 16)
        self.lane_blocks = chips // self.row_blocks
        self.height = rows // self.row_blocks
        self.width = self.half // self.lane_blocks
        self.tall = self.height * self.width // LANES


def exchanges(order, depth):
    deep = [("z", 1 << i) for i in reversed(range(depth.bit_length() - 1))]
    bits = {"x": [("x", 1)], "y": [("y", 1)], "z": deep}
    return [sum((bits[axis] for axis in axes), []) for axes in order]


def relative(core, place, chip, depth, order):
    differ = dict(zip("xyz", (a ^ b for a, b in zip(place, chip))))
    found = []
    for bits in exchanges(order, depth):
        at = 0
        for axis, bit in bits:
            at = at * 2 + ((differ[axis] & bit) // bit)
        found.append(at)
    return jnp.where(core == 0, *found)


def chip_of(index, depth):
    return index // (2 * depth), (index // depth) % 2, index % depth


def absolute(core, place, index, depth, order):
    flips = []
    for bits in exchanges(order, depth):
        flip = dict.fromkeys("xyz", 0)
        for i, (axis, bit) in enumerate(reversed(bits)):
            flip[axis] |= bit * ((index >> i) & 1)
        flips.append(flip)
    x, y, z = (
        at ^ jnp.where(core == 0, flips[0][axis], flips[1][axis]) for axis, at in zip("xyz", place)
    )
    return (x * 2 + y) * depth + z % depth


def store_pieces(out_ref, core, place, depth, order, pieces, base, value, row_start):
    for first in range(0, value.shape[0], pieces.height):
        row_block = (row_start + first) // pieces.height
        for lane_block in range(pieces.lane_blocks):
            index = row_block * pieces.lane_blocks + lane_block
            rel = relative(core, place, chip_of(index, depth), depth, order)
            for j in range(pieces.width // LANES):
                at = base + j * pieces.height
                lane = lane_block * pieces.width + j * LANES
                out_ref[rel, at : at + pieces.height, :] = value[
                    first : first + pieces.height, lane : lane + LANES
                ].astype(BF16)


def weight_grad(keep_ref, send_ref, core, place, depth, order, pieces, base, lhs, rhs_ref):
    stripe = max(pieces.height, min(512, pieces.rows))
    for out_ref, owner in ((send_ref, core ^ 1), (keep_ref, core)):
        rhs = rhs_ref[:, pl.ds(pl.multiple_of(owner * pieces.half, LANES), pieces.half)]
        for start in range(0, pieces.rows, stripe):
            value = dot_tn(lhs[:, start : start + stripe], rhs)
            store_pieces(out_ref, owner, place, depth, order, pieces, base, value, start)


def place_of():
    dp, blk = lax.axis_index("dp"), lax.axis_index("blk")
    return blk % 2, (blk // 2, dp % 2, dp // 2), blk


def fetch(sems, *pairs):
    copies = [pltpu.make_async_copy(a, b, sems.at[i]) for i, (a, b) in enumerate(pairs)]
    for copy in copies:
        copy.start()
    return [copy.wait for copy in copies]


def flag_column(flags, at):
    share = flags.shape[2]
    eye = lax.broadcasted_iota(jnp.int32, (share, share), 0) == lax.broadcasted_iota(
        jnp.int32, (share, share), 1
    )
    return jnp.sum(jnp.where(eye, flags[at], 0), axis=1, keepdims=True) == 1


def fill_kernel(count, tokens_hbm, cotangent_hbm, flags_hbm, mask_hbm, *refs):
    outs, cots = refs[:count], refs[count : 2 * count]
    tokens, cotangent, flags, mask_token, sems = refs[2 * count :]
    waits = fetch(
        sems,
        (tokens_hbm, tokens),
        (flags_hbm, flags),
        (mask_hbm, mask_token),
        (cotangent_hbm, cotangent),
    )
    for wait in waits[:3]:
        wait()
    blk = lax.axis_index("blk")
    share = tokens.shape[1]
    for k in range(count):
        at = blk ^ k
        outs[k][...] = jnp.where(
            flag_column(flags, at), row(mask_token), tokens[at].astype(F32)
        ).astype(BF16)
    waits[3]()
    for k in range(count):
        at = blk ^ k
        cots[k][:share, :] = cotangent[at]
        cots[k][share:, :] = jnp.zeros((16, cots[k].shape[1]), BF16)
        first = lax.broadcasted_iota(jnp.int32, (16, share), 0) == 0
        flag = (flags[at] == 1).astype(F32)
        cots[k][share:, :share] = jnp.where(first, flag, 0.0).astype(BF16)


GAIN1, BIAS1, B_QUERY, B_VALUE, B_OUT, GAIN2, BIAS2, B_DOWN, B_UP = range(9)
QUOTA = 15


def prefetch_kernel(images, weight_hbm, buckets_hbm, *refs):
    count = (len(refs) - 4) // 2
    weight, vecs = refs[count : count + 2]
    held, buckets, sems = refs[count + 2 : -2], refs[-2], refs[-1]
    waits = fetch(
        sems, (weight_hbm, weight), (buckets_hbm, buckets), *zip(refs[:count], held)
    )
    for wait in waits[1:]:
        wait()
    width = vecs.shape[1]
    vecs[...] = jnp.zeros(vecs.shape, F32)
    line = 0
    for ref in held:
        for at in range(0, ref.shape[0], width):
            vecs[line : line + 1, :] = row(ref)[:, at : at + width]
            line += 1
    micro = lax.axis_index("blk") // images
    quota = jnp.zeros((1, 1), jnp.int32)
    for m in range(buckets.shape[1]):
        bucket = buckets[:, m : m + 1]
        here = jnp.where(bucket == 0, 25, jnp.where(bucket == 1, 49, 64))
        quota = quota + jnp.where(micro == m, here, 0)
    vecs[QUOTA : QUOTA + 1, :] = jnp.broadcast_to(quota.astype(F32), (1, width))
    waits[0]()


def vector(rows, which):
    return rows[which : which + 1, :]


def forward_kernel(count, share, *refs):
    sources, refs = refs[:3], refs[3:]
    xs, refs = refs[:count], refs[count:]
    vecs, w_qkv = refs[:2]
    targets = refs[2:5]
    qkv_ref, p_ref, rinv_ref, o_ref, x2_ref, n2_ref, h_ref, gp_ref, sems = refs[5:]
    waits = fetch(sems, *zip(sources, targets))
    w_out, w_up, _ = targets
    quota = vecs[QUOTA : QUOTA + 1, 0:1].astype(jnp.int32)
    width = xs[0].shape[1]
    head = width // HEADS
    rows = count * share
    x = jnp.concatenate([ref[...] for ref in xs], axis=0).astype(F32)
    xhat, _ = norm_stats(x)
    n1 = (xhat * vector(vecs, GAIN1) + vector(vecs, BIAS1)).astype(BF16)
    for part in range(3):
        cols = slice(part * width, (part + 1) * width)
        value = dot(n1, w_qkv[:, cols])
        if part == 0:
            value = value + vector(vecs, B_QUERY)
        if part == 2:
            value = value + vector(vecs, B_VALUE)
        qkv_ref[:, cols] = value.astype(BF16)
    key = lax.broadcasted_iota(jnp.int32, (rows, 1), 0)
    dead = jnp.where(key % share < quota, 0.0, -1e30).astype(F32)
    lane_head = lax.broadcasted_iota(jnp.int32, (1, LANES), 1) // head
    scale = head ** (-0.5) * LOG2E
    per = LANES // head
    ones = jnp.ones((rows, LANES), BF16)
    for group in range(width // LANES):
        at = group * LANES
        q = qkv_ref[:, at : at + LANES]
        keys = qkv_ref[:, width + at : width + at + LANES]
        values = jnp.concatenate(
            [qkv_ref[:, 2 * width + at : 2 * width + at + LANES], ones], axis=1
        )
        acc = jnp.zeros((rows, LANES), F32)
        racc = jnp.zeros((rows, LANES), F32)
        for i in range(per):
            here = lane_head == i
            s = dot_nt(keys * here.astype(F32).astype(BF16), q) * scale + dead
            top = jnp.max(s, axis=0, keepdims=True)
            p = jnp.exp2(s - top).astype(BF16)
            p_ref[group * per + i] = p
            both = dot_tn(p, values)
            rinv = 1.0 / both[:, LANES:]
            acc = jnp.where(here, both[:, :LANES] * rinv, acc)
            racc = jnp.where(here, rinv, racc)
        o_ref[:, at : at + LANES] = acc.astype(BF16)
        rinv_ref[:, at : at + LANES] = racc
    waits[0]()
    x2 = x + (dot(o_ref[...], w_out[...]) + vector(vecs, B_OUT))
    x2_ref[...] = x2
    xhat2, _ = norm_stats(x2)
    n2 = (xhat2 * vector(vecs, GAIN2) + vector(vecs, BIAS2)).astype(BF16)
    n2_ref[...] = n2
    hidden = w_up.shape[1]
    step = width
    waits[1]()
    for start in range(0, hidden, step):
        cols = slice(start, start + step)
        u = dot(n2, w_up[:, cols]) + vector(vecs, B_UP + start // step)
        cdf = 0.5 + 0.5 * lax.erf(u * (0.5**0.5))
        pdf = jnp.exp(-0.5 * u * u) * 0.3989422804014327
        h_ref[:, cols] = (u * cdf).astype(BF16)
        gp_ref[:, cols] = (cdf + u * pdf).astype(BF16)
    waits[2]()


def down_kernel(depth, order, down, count, share, *refs):
    cs, (vecs, h_ref, g_ref, keep_ref, send_ref) = refs[:count], refs[count:]
    core, place, _ = place_of()
    quota = vecs[QUOTA : QUOTA + 1, 0:1].astype(jnp.int32)
    live_rows = lax.broadcasted_iota(jnp.int32, (share, 1), 0) < quota
    for k in range(count):
        g_ref[k * share : (k + 1) * share, :] = jnp.where(
            live_rows, cs[k][:share, :].astype(F32), 0.0
        ).astype(BF16)
    weight_grad(keep_ref, send_ref, core, place, depth, order, down, 0, h_ref, g_ref)


def middle_kernel(
    depth,
    order,
    up,
    after,
    g_ref, gp_ref, h_ref, n2_ref, o_ref, x2_ref, vecs, w_up, w_down,
    keep_ref, send_ref, dx2_ref, dx2r_ref, out_ref, small_ref, du_ref,
):
    core, place, _ = place_of()
    g = g_ref[...]
    hidden = w_up.shape[1]
    width = g.shape[1]
    step = 512
    small_ref[...] = jnp.zeros(small_ref.shape, F32)
    dn2 = jnp.zeros((g.shape[0], width), F32)
    for start in range(0, hidden, step):
        cols = slice(start, start + step)
        dh = dot_nt(g, w_down[cols, :])
        du = (dh * gp_ref[:, cols].astype(F32)).astype(BF16)
        du_ref[:, cols] = du
        small_ref[0:1, cols] = jnp.sum(du.astype(F32), axis=0, keepdims=True)
        dn2 = dn2 + dot_nt(du, w_up[:, cols])
    x2 = x2_ref[...]
    xhat, rstd = norm_stats(x2)
    gf = g.astype(F32)
    dx2 = gf + norm_back(dn2, xhat, rstd, vector(vecs, GAIN2))
    dx2_ref[...] = dx2
    dx2r = dx2.astype(BF16)
    dx2r_ref[...] = dx2r
    small_ref[1:2, 0:width] = jnp.sum(dx2r.astype(F32), axis=0, keepdims=True)
    small_ref[1:2, width : 2 * width] = jnp.sum(dn2 * xhat, axis=0, keepdims=True)
    small_ref[1:2, 2 * width : 3 * width] = jnp.sum(dn2, axis=0, keepdims=True)
    small_ref[1:2, 3 * width : 4 * width] = jnp.sum(gf, axis=0, keepdims=True)
    weight_grad(keep_ref, send_ref, core, place, depth, order, up, 0, n2_ref, du_ref)
    weight_grad(keep_ref, send_ref, core, place, depth, order, after, up.tall, o_ref, dx2r_ref)
    out_ref[...] = (x2 + (dot(h_ref[...], w_down[...]) + vector(vecs, B_DOWN))).astype(BF16)


def backward_kernel(
    depth,
    order,
    proj,
    count,
    share,
    *refs,
):
    refs = list(refs)
    xs = [refs.pop(0) for _ in range(count)]
    cs = [refs.pop(0) for _ in range(count)]
    qkv_ref, p_ref, rinv_ref, o_ref, dx2_ref, dx2r_ref, block_ref, sub_ref, vecs, w_qkv, w_out = refs[:11]
    refs = refs[11:]
    results = [refs.pop(0) for _ in range(count)]
    keep_ref, send_ref, dqkv_ref, small = refs
    core, place, _ = place_of()
    rows = count * share
    width = xs[0].shape[1]
    head = width // HEADS
    per = LANES // head
    d_o = dot_nt(dx2r_ref[...], w_out[...]).astype(BF16).astype(F32)
    d_scaled = d_o * rinv_ref[...]
    product = (d_scaled * o_ref[...].astype(F32)).astype(BF16)
    d_scaled = d_scaled.astype(BF16)
    lane_head = lax.broadcasted_iota(jnp.int32, (1, LANES), 1) // head
    minus = jnp.full((rows, LANES), -1.0, BF16)
    scale = head ** (-0.5)
    for group in range(width // LANES):
        at = group * LANES
        q = qkv_ref[:, at : at + LANES]
        keys = qkv_ref[:, width + at : width + at + LANES]
        values = qkv_ref[:, 2 * width + at : 2 * width + at + LANES]
        ds_o = d_scaled[:, at : at + LANES]
        rhs = jnp.concatenate([ds_o, product[:, at : at + LANES]], axis=1)
        dq = jnp.zeros((rows, LANES), F32)
        dk = jnp.zeros((rows, LANES), F32)
        dv = jnp.zeros((rows, LANES), F32)
        for i in range(per):
            here = lane_head == i
            mask = here.astype(F32).astype(BF16)
            lhs = jnp.concatenate([values * mask, minus * mask], axis=1)
            p = p_ref[group * per + i]
            ds = (p.astype(F32) * dot_nt(lhs, rhs)).astype(BF16)
            dq = jnp.where(here, dot_tn(ds, keys), dq)
            dk = jnp.where(here, dot(ds, q), dk)
            dv = jnp.where(here, dot(p, ds_o), dv)
        dqkv_ref[:, at : at + LANES] = (dq * scale).astype(BF16)
        dqkv_ref[:, width + at : width + at + LANES] = (dk * scale).astype(BF16)
        dqkv_ref[:, 2 * width + at : 2 * width + at + LANES] = dv.astype(BF16)
    x = jnp.concatenate([ref[...] for ref in xs], axis=0).astype(F32)
    xhat, rstd = norm_stats(x)
    gain = vector(vecs, GAIN1)
    n1 = (xhat * gain + vector(vecs, BIAS1)).astype(BF16)
    weight_grad(keep_ref, send_ref, core, place, depth, order, proj, 0, n1, dqkv_ref)
    dn1 = dot_nt(dqkv_ref[...], w_qkv[...])
    dx = (dx2_ref[...] + norm_back(dn1, xhat, rstd, gain)).astype(BF16)
    d_mask = jnp.zeros((16, width), F32)
    for k in range(count):
        part = dx[k * share : (k + 1) * share, :]
        d_mask = d_mask + dot(cs[k][share : share + 16, :share], part)
        results[k][:share, :] = block_ref[k * share : (k + 1) * share, :]
        results[k][share:, :] = part
    blocks = small.shape[0]
    small[...] = jnp.zeros(small.shape, F32)
    wide = [
        d_mask[0:1, :],
        jnp.sum(dn1 * xhat, axis=0, keepdims=True),
        jnp.sum(dn1, axis=0, keepdims=True),
        jnp.sum(dqkv_ref[:, :width].astype(F32), axis=0, keepdims=True),
        jnp.sum(dqkv_ref[:, 2 * width :].astype(F32), axis=0, keepdims=True),
        sub_ref[1:2, :],
        sub_ref[0:1, :],
    ]
    lines = [v[:, j : j + LANES] for v in wide for j in range(0, v.shape[1], LANES)]
    each = -(-len(lines) // blocks)
    for i, line in enumerate(lines):
        small[i // each, i % each : i % each + 1, :] = line
    chips = blocks // 2
    for out_ref, owner in ((send_ref, core ^ 1), (keep_ref, core)):
        for index in range(chips):
            rel = relative(owner, place, chip_of(index, depth), depth, order)
            out_ref[rel, proj.tall : proj.tall + 16, :] = small[owner * chips + index].astype(BF16)


def gather_kernel(depth, order, layout, scale, small_at, sizes, *refs):
    count = len(layout)
    halves, outs = refs[:4], refs[4 : 4 + count]
    vectors = refs[4 + count : 4 + count + len(sizes)]
    held = refs[4 + count + len(sizes) : -2]
    small, sems = refs[-2:]
    core, place, _ = place_of()
    half = halves[0].shape[0]
    chips = 2 * half
    copies = []
    for side, owner in ((0, core), (1, core ^ 1)):
        for rel in range(chips):
            ref, at_block = halves[2 * side + rel // half], rel % half
            index = absolute(owner, place, rel, depth, order)
            slot = side * chips + rel
            for which, (pieces, base) in enumerate(layout):
                for j in range(pieces.width // LANES):
                    at = base + j * pieces.height
                    held[which][slot, :, j * LANES : (j + 1) * LANES] = (
                        ref[at_block, at : at + pieces.height, :].astype(F32) * scale
                    )
                top = pl.multiple_of((index // pieces.lane_blocks) * pieces.height, 16)
                lane = owner * pieces.half + (index % pieces.lane_blocks) * pieces.width
                copy = pltpu.make_async_copy(
                    held[which].at[slot],
                    outs[which].at[
                        pl.ds(top, pieces.height),
                        pl.ds(pl.multiple_of(lane, LANES), pieces.width),
                    ],
                    sems.at[which, slot],
                )
                copy.start()
                copies.append(copy)
            if sizes:
                small[owner * chips + index] = (
                    ref[at_block, small_at : small_at + 16, :].astype(F32) * scale
                )
    lines = sum(sizes) // LANES
    each = max(1, -(-lines // (2 * chips)))
    line = 0
    for out, size in zip(vectors, sizes):
        for j in range(size // LANES):
            out[j * LANES : (j + 1) * LANES] = small[
                line // each, line % each : line % each + 1, :
            ].reshape(LANES)
            line += 1
    for copy in copies:
        copy.wait()


def finish_kernel(flags, *refs):
    block_out, token_grad = refs[-2:]
    share = block_out.shape[1]
    blk = lax.axis_index("blk")
    for k, ref in enumerate(refs[:-2]):
        at = blk ^ k
        block_out[at] = ref[:share, :]
        token_grad[at] = jnp.where(flag_column(flags, at), 0.0, ref[share:, :].astype(F32))


WHOLE = pl.BlockSpec(memory_space=pltpu.VMEM)
FAR = pl.BlockSpec(memory_space=pltpu.HBM)


def call(kernel, outs, *args, scratch=(), far=0, far_outs=0, name=None):
    args = list(args)
    for i in range(far):
        args[i] = pltpu.with_memory_space_constraint(args[i], pltpu.HBM)
    return pl.pallas_call(
        kernel,
        out_shape=tuple(outs),
        in_specs=[FAR] * far + [WHOLE] * (len(args) - far),
        out_specs=tuple([FAR] * far_outs + [WHOLE] * (len(outs) - far_outs)),
        scratch_shapes=list(scratch),
        compiler_params=pltpu.CompilerParams(vmem_limit_bytes=VMEM_LIMIT),
        cost_estimate=pl.CostEstimate(
            flops=int(US.get(name, 0) * 1.15e9), bytes_accessed=0, transcendentals=0
        ),
        name=name,
    )(*args)


def like(array):
    return pltpu.VMEM(array.shape, array.dtype)


def after(value, *others):
    return lax.optimization_barrier((value, *others))[0]


def shape(dims, kind=BF16):
    return jax.ShapeDtypeStruct(tuple(dims), kind)


def add(*parts):
    total = parts[0].astype(F32)
    for part in parts[1:]:
        total = total + part.astype(F32)
    return total.astype(BF16)


def shards(
    dp_size,
    blk_size,
    tokens,
    mask_flags,
    buckets,
    cotangent,
    mask_token,
    norm1_gain,
    norm1_bias,
    w_qkv,
    b_query,
    b_value,
    w_out,
    b_out,
    norm2_gain,
    norm2_bias,
    w_up,
    b_up,
    w_down,
    b_down,
):
    micro_count, images, share, width = tokens.shape
    hidden = w_up.shape[1]
    count = micro_count * images
    rows = count * share
    deep = dp_size // 2
    depth = deep // 2
    chips = 4 * depth
    total_images = float(micro_count * images * dp_size)

    def send(value, change):
        table = []
        for d in range(dp_size):
            for b in range(blk_size):
                nz, ny, nx, nc = change(d // 2, d % 2, b // 2, b % 2)
                table.append((d * blk_size + b, (nz * 2 + ny) * blk_size + nx * 2 + nc))
        return lax.ppermute(value, ("dp", "blk"), table)

    def core_pair(z, y, x, c):
        return z, y, x, c ^ 1

    def depth_pair(k):
        return lambda z, y, x, c: (z ^ k, y, x, c)

    def image_pair(k):
        return lambda z, y, x, c: (z, y, x ^ (k >> 1), c ^ (k & 1))

    def halving(order):
        def flip(bits):
            def change(z, y, x, c):
                axis, bit = bits[c]
                at = {"z": z, "y": y, "x": x}
                at[axis] ^= bit
                return at["z"], at["y"], at["x"], c

            return change

        return [flip(bits) for bits in zip(*exchanges(order, depth))]

    class Sum:
        def __init__(self, keep, sent, order):
            self.order = order
            self.pairs = halving(order)
            self.keep, self.sent = keep, sent
            self.step = 0

        def cores(self, *behind):
            self.got = send(after(self.sent, *behind) if behind else self.sent, core_pair)
            return self

        def advance(self, *behind):
            count = len(self.pairs)
            if self.step < count:
                half = self.keep.shape[0] // 2
                away = add(self.keep[half:], self.got[half:])
                self.keep = add(self.keep[:half], self.got[:half])
                change = self.pairs[self.step]
            elif self.step == count:
                away = self.keep = add(self.keep, self.got)
                change = depth_pair(depth)
            else:
                if self.step == count + 1:
                    self.keep = add(self.keep, self.got)
                else:
                    self.keep = jnp.concatenate([self.keep, self.got])
                away = self.keep
                change = self.pairs[2 * count - self.step]
            self.got = send(after(away, *behind) if behind else away, change)
            self.step += 1

        @property
        def left(self):
            return 2 * len(self.pairs) + 1 - self.step

        def finish(self):
            mine = (self.keep, self.got)
            return mine + tuple(send(a, core_pair) for a in mine)

    down = Pieces(hidden, width, chips)
    up = Pieces(width, hidden, chips)
    out = Pieces(width, width, chips)
    proj = Pieces(width, 3 * width, chips)
    dma = pltpu.SemaphoreType.DMA

    tokens_in = tokens.reshape(count, share, width)
    flags = mask_flags.reshape(count, 1, share)
    cots_in = cotangent.reshape(count, share, width)
    filled = call(
        functools.partial(fill_kernel, count),
        [shape((share, width))] * count + [shape((share + 16, width))] * count,
        tokens_in,
        cots_in,
        flags,
        mask_token,
        far=4,
        scratch=[like(tokens_in), like(cots_in), like(flags), like(mask_token), dma((4,))],
        name="fill",
    )
    xs = list(filled[:1]) + [send(filled[k], image_pair(k)) for k in range(1, count)]
    cs = [filled[count]] + [
        send(after(filled[count + k], xs[1]), image_pair(k)) for k in range(1, count)
    ]
    vectors = [norm1_gain, norm1_bias, b_query, b_value, b_out, norm2_gain, norm2_bias, b_down, b_up]
    w_qkv, vecs = call(
        functools.partial(prefetch_kernel, images),
        [shape(w_qkv.shape), shape((16, width), F32)],
        after(w_qkv, xs[1]),
        buckets.T,
        *vectors,
        far=2 + len(vectors),
        scratch=[like(v) for v in vectors] + [like(buckets.T), dma((2 + len(vectors),))],
        name="prefetch",
    )
    weights = [w_out, w_up, w_down]
    w_out, w_up, w_down, qkv, p, rinv, o, x2, n2, h, gp = call(
        functools.partial(forward_kernel, count, share),
        [shape(w.shape) for w in weights]
        + [
            shape((rows, 3 * width)),
            shape((HEADS, rows, rows)),
            shape((rows, width), F32),
            shape((rows, width)),
            shape((rows, width), F32),
            shape((rows, width)),
            shape((rows, hidden)),
            shape((rows, hidden)),
        ],
        *weights,
        *xs,
        vecs,
        w_qkv,
        far=len(weights),
        scratch=[dma((len(weights),))],
        name="forward",
    )
    g, keep, sent = call(
        functools.partial(down_kernel, depth, ORDERS[0], down, count, share),
        [shape((rows, width))] + [shape((chips, down.tall, LANES))] * 2,
        *cs,
        vecs,
        h,
        name="down",
    )
    one = Sum(keep, sent, ORDERS[0]).cores()
    keep, sent, dx2, dx2r, block, sub = call(
        functools.partial(middle_kernel, depth, ORDERS[1], up, out),
        [shape((chips, up.tall + out.tall, LANES))] * 2
        + [
            shape((rows, width), F32),
            shape((rows, width)),
            shape((rows, width)),
            shape((8, hidden), F32),
        ],
        g,
        gp,
        h,
        n2,
        o,
        x2,
        vecs,
        w_up,
        w_down,
        scratch=[pltpu.VMEM((rows, hidden), BF16)],
        name="middle",
    )
    dx2r = after(dx2r, one.got)
    two = Sum(keep, sent, ORDERS[1]).cores()
    one.advance()
    *results, keep, sent = call(
        functools.partial(backward_kernel, depth, ORDERS[2], proj, count, share),
        [shape((2 * share, width))] * count + [shape((chips, proj.tall + 16, LANES))] * 2,
        *xs,
        *cs,
        qkv,
        p,
        rinv,
        o,
        dx2,
        dx2r,
        block,
        sub,
        vecs,
        w_qkv,
        w_out,
        scratch=[
            pltpu.VMEM((rows, 3 * width), BF16),
            pltpu.VMEM((2 * chips, 16, LANES), F32),
        ],
        name="backward",
    )
    three = Sum(keep, sent, ORDERS[2])
    three.cores(two.got)
    def whole(group, layout, small_at=0, sizes=(), name=None):
        outs = [shape((p.rows, 2 * p.half), F32) for p, _ in layout]
        outs += [shape((n,), F32) for n in sizes]
        return call(
            functools.partial(
                gather_kernel, depth, group.order, layout, 1.0 / total_images, small_at, sizes
            ),
            outs,
            *group.finish(),
            far_outs=len(layout),
            scratch=[pltpu.VMEM((2 * chips, p.height, p.width), F32) for p, _ in layout]
            + [pltpu.VMEM((2 * chips, 16, LANES), F32), dma((len(layout), 2 * chips))],
            name=name,
        )

    groups = (one, two, three)
    layouts = ([(down, 0)], [(up, 0), (out, up.tall)], [(proj, 0)])
    names = ("gather_down", "gather_up", "gather_proj")
    sizes = (width,) * 9 + (hidden,)
    done = {(3, 0): keep, (0, 0): one.got}
    grads = {}
    progress = True
    while progress:
        progress = False
        for which in (2, 1, 0):
            group = groups[which]
            if which in grads:
                continue
            waits = [b for a, b in TIES if a == (which, group.step)]
            waits += [(4, b) for a, b in WRITTEN if a == (which, group.step)]
            if any(w not in done for w in waits):
                continue
            progress = True
            behind = [done[w] for w in waits]
            if group.left:
                group.advance(*behind)
                done[which, group.step - 1] = group.got
            else:
                if behind:
                    group.got = after(group.got, *behind)
                grads[which] = whole(
                    group,
                    layouts[which],
                    proj.tall if which == 2 else 0,
                    sizes if which == 2 else (),
                    name=names[which],
                )
                done[4, which] = grads[which][0]
        if (5, 0) not in done and RESULTS in done:
            results = [results[0]] + [
                send(after(results[k], done[RESULTS]), image_pair(k)) for k in range(1, count)
            ]
            done[5, 0] = results[-1]
            progress = True
    (grad_down,), (grad_up, grad_out), (grad_proj, *small) = (grads[i] for i in range(3))
    mask_g, gain1_g, bias1_g, query_g, value_g, after_g, gain2_g, bias2_g, reduce_g, expand_g = small

    block_out, token_grad = call(
        finish_kernel,
        [shape((count, share, width)), shape((count, share, width), F32)],
        flags,
        *results,
        name="finish",
    )
    return (
        block_out.reshape(tokens.shape),
        token_grad.reshape(tokens.shape),
        mask_g,
        gain1_g,
        bias1_g,
        grad_proj,
        query_g,
        value_g,
        grad_out,
        after_g,
        gain2_g,
        bias2_g,
        grad_up,
        expand_g,
        grad_down,
        reduce_g,
    )


def solution(mesh):
    rows = P(None, "dp", "blk", None)
    placed = (rows, P(None, "dp", "blk"), P(None, "dp"), rows) + (P(),) * 14
    return jax.shard_map(
        functools.partial(shards, mesh.shape["dp"], mesh.shape["blk"]),
        mesh=mesh,
        in_specs=placed,
        out_specs=(rows, rows) + (P(),) * 14,
        check_vma=False,
    )
```

```python
import functools

import jax
import jax.numpy as jnp
from jax import lax
from jax.experimental import pallas as pl
from jax.experimental.pallas import tpu as pltpu
from jax.sharding import PartitionSpec as P

HEADS = 16
LANES = 128
EPS = 1e-06
LOG2E = 1.4426950408889634
BF16 = jnp.bfloat16
F32 = jnp.float32
ORDERS = (('zxy', 'yxz'), ('yzx', 'zxy'), ('yzx', 'xzy'))
TIES = (((2, 2), (5, 0)), ((0, 2), (1, 0)), ((1, 3), (0, 1)), ((0, 1), (3, 0)), ((2, 4), (1, 4)), ((0, 6), (1, 5)), ((2, 5), (1, 2)), ((2, 1), (3, 0)), ((2, 2), (0, 1)), ((0, 2), (3, 0)), ((2, 3), (1, 2)), ((1, 0), (3, 0)))
RESULTS = (1, 2)
WRITTEN = ()
BEFORE = 1
THIRD = 1
US = {'forward': 15, 'gather_up': 3}
VMEM_LIMIT = 24 * 1024 * 1024


def dot(a, b):
    return jnp.dot(a, b, preferred_element_type=F32)


def dot_nt(a, b):
    return lax.dot_general(a, b, (((1,), (1,)), ((), ())), preferred_element_type=F32)


def dot_tn(a, b):
    return lax.dot_general(a, b, (((0,), (0,)), ((), ())), preferred_element_type=F32)


def row(ref):
    return ref[...].astype(F32).reshape(1, -1)


def norm_stats(rows):
    centre = jnp.mean(rows, axis=-1, keepdims=True)
    centred = rows - centre
    spread = jnp.mean(centred * centred, axis=-1, keepdims=True)
    rstd = lax.rsqrt(spread + EPS)
    return centred * rstd, rstd


def norm_back(grad_normed, xhat, rstd, gain):
    grad_xhat = grad_normed * gain
    first = jnp.mean(grad_xhat, axis=-1, keepdims=True)
    second = jnp.mean(grad_xhat * xhat, axis=-1, keepdims=True)
    return rstd * (grad_xhat - first - xhat * second)


class Pieces:
    def __init__(self, rows, cols, chips):
        self.rows = rows
        self.half = cols // 2
        self.row_blocks = min(chips, rows // 16)
        self.lane_blocks = chips // self.row_blocks
        self.height = rows // self.row_blocks
        self.width = self.half // self.lane_blocks
        self.tall = self.height * self.width // LANES


def exchanges(order, depth):
    deep = [("z", 1 << i) for i in reversed(range(depth.bit_length() - 1))]
    bits = {"x": [("x", 1)], "y": [("y", 1)], "z": deep}
    return [sum((bits[axis] for axis in axes), []) for axes in order]


def relative(core, place, chip, depth, order):
    differ = dict(zip("xyz", (a ^ b for a, b in zip(place, chip))))
    found = []
    for bits in exchanges(order, depth):
        at = 0
        for axis, bit in bits:
            at = at * 2 + ((differ[axis] & bit) // bit)
        found.append(at)
    return jnp.where(core == 0, *found)


def chip_of(index, depth):
    return index // (2 * depth), (index // depth) % 2, index % depth


def absolute(core, place, index, depth, order):
    flips = []
    for bits in exchanges(order, depth):
        flip = dict.fromkeys("xyz", 0)
        for i, (axis, bit) in enumerate(reversed(bits)):
            flip[axis] |= bit * ((index >> i) & 1)
        flips.append(flip)
    x, y, z = (
        at ^ jnp.where(core == 0, flips[0][axis], flips[1][axis]) for axis, at in zip("xyz", place)
    )
    return (x * 2 + y) * depth + z % depth


def store_pieces(out_ref, core, place, depth, order, pieces, base, value, row_start):
    for first in range(0, value.shape[0], pieces.height):
        row_block = (row_start + first) // pieces.height
        for lane_block in range(pieces.lane_blocks):
            index = row_block * pieces.lane_blocks + lane_block
            rel = relative(core, place, chip_of(index, depth), depth, order)
            for j in range(pieces.width // LANES):
                at = base + j * pieces.height
                lane = lane_block * pieces.width + j * LANES
                out_ref[rel, at : at + pieces.height, :] = value[
                    first : first + pieces.height, lane : lane + LANES
                ].astype(BF16)


def weight_grad(keep_ref, send_ref, core, place, depth, order, pieces, base, lhs, rhs_ref):
    stripe = max(pieces.height, min(512, pieces.rows))
    for out_ref, owner in ((send_ref, core ^ 1), (keep_ref, core)):
        rhs = rhs_ref[:, pl.ds(pl.multiple_of(owner * pieces.half, LANES), pieces.half)]
        for start in range(0, pieces.rows, stripe):
            value = dot_tn(lhs[:, start : start + stripe], rhs)
            store_pieces(out_ref, owner, place, depth, order, pieces, base, value, start)


def place_of():
    dp, blk = lax.axis_index("dp"), lax.axis_index("blk")
    return blk % 2, (blk // 2, dp % 2, dp // 2), blk


def fetch(sems, *pairs):
    copies = [pltpu.make_async_copy(a, b, sems.at[i]) for i, (a, b) in enumerate(pairs)]
    for copy in copies:
        copy.start()
    return [copy.wait for copy in copies]


def flag_column(flags, at):
    share = flags.shape[2]
    eye = lax.broadcasted_iota(jnp.int32, (share, share), 0) == lax.broadcasted_iota(
        jnp.int32, (share, share), 1
    )
    return jnp.sum(jnp.where(eye, flags[at], 0), axis=1, keepdims=True) == 1


def fill_kernel(count, tokens_hbm, cotangent_hbm, flags_hbm, mask_hbm, *refs):
    outs, cots = refs[:count], refs[count : 2 * count]
    tokens, cotangent, flags, mask_token, sems = refs[2 * count :]
    waits = fetch(
        sems,
        (tokens_hbm, tokens),
        (flags_hbm, flags),
        (mask_hbm, mask_token),
        (cotangent_hbm, cotangent),
    )
    for wait in waits[:3]:
        wait()
    blk = lax.axis_index("blk")
    share = tokens.shape[1]
    for k in range(count):
        at = blk ^ k
        outs[k][...] = jnp.where(
            flag_column(flags, at), row(mask_token), tokens[at].astype(F32)
        ).astype(BF16)
    waits[3]()
    for k in range(count):
        at = blk ^ k
        cots[k][:share, :] = cotangent[at]
        cots[k][share:, :] = jnp.zeros((16, cots[k].shape[1]), BF16)
        first = lax.broadcasted_iota(jnp.int32, (16, share), 0) == 0
        flag = (flags[at] == 1).astype(F32)
        cots[k][share:, :share] = jnp.where(first, flag, 0.0).astype(BF16)


GAIN1, BIAS1, B_QUERY, B_VALUE, B_OUT, GAIN2, BIAS2, B_DOWN, B_UP = range(9)
QUOTA = 15


def prefetch_kernel(images, weight_hbm, buckets_hbm, *refs):
    count = (len(refs) - 4) // 2
    weight, vecs = refs[count : count + 2]
    held, buckets, sems = refs[count + 2 : -2], refs[-2], refs[-1]
    waits = fetch(
        sems, (weight_hbm, weight), (buckets_hbm, buckets), *zip(refs[:count], held)
    )
    for wait in waits[1:]:
        wait()
    width = vecs.shape[1]
    vecs[...] = jnp.zeros(vecs.shape, F32)
    line = 0
    for ref in held:
        for at in range(0, ref.shape[0], width):
            vecs[line : line + 1, :] = row(ref)[:, at : at + width]
            line += 1
    micro = lax.axis_index("blk") // images
    quota = jnp.zeros((1, 1), jnp.int32)
    for m in range(buckets.shape[1]):
        bucket = buckets[:, m : m + 1]
        here = jnp.where(bucket == 0, 25, jnp.where(bucket == 1, 49, 64))
        quota = quota + jnp.where(micro == m, here, 0)
    vecs[QUOTA : QUOTA + 1, :] = jnp.broadcast_to(quota.astype(F32), (1, width))
    waits[0]()


def vector(rows, which):
    return rows[which : which + 1, :]


def forward_kernel(count, share, *refs):
    sources, refs = refs[:3], refs[3:]
    xs, refs = refs[:count], refs[count:]
    vecs, w_qkv = refs[:2]
    targets = refs[2:5]
    qkv_ref, p_ref, rinv_ref, o_ref, x2_ref, n2_ref, h_ref, gp_ref, sems = refs[5:]
    waits = fetch(sems, *zip(sources, targets))
    w_out, w_up, _ = targets
    quota = vecs[QUOTA : QUOTA + 1, 0:1].astype(jnp.int32)
    width = xs[0].shape[1]
    head = width // HEADS
    rows = count * share
    x = jnp.concatenate([ref[...] for ref in xs], axis=0).astype(F32)
    xhat, _ = norm_stats(x)
    n1 = (xhat * vector(vecs, GAIN1) + vector(vecs, BIAS1)).astype(BF16)
    for part in range(3):
        cols = slice(part * width, (part + 1) * width)
        value = dot(n1, w_qkv[:, cols])
        if part == 0:
            value = value + vector(vecs, B_QUERY)
        if part == 2:
            value = value + vector(vecs, B_VALUE)
        qkv_ref[:, cols] = value.astype(BF16)
    key = lax.broadcasted_iota(jnp.int32, (rows, 1), 0)
    dead = jnp.where(key % share < quota, 0.0, -1e30).astype(F32)
    lane_head = lax.broadcasted_iota(jnp.int32, (1, LANES), 1) // head
    scale = head ** (-0.5) * LOG2E
    per = LANES // head
    ones = jnp.ones((rows, LANES), BF16)
    for group in range(width // LANES):
        at = group * LANES
        q = qkv_ref[:, at : at + LANES]
        keys = qkv_ref[:, width + at : width + at + LANES]
        values = jnp.concatenate(
            [qkv_ref[:, 2 * width + at : 2 * width + at + LANES], ones], axis=1
        )
        acc = jnp.zeros((rows, LANES), F32)
        racc = jnp.zeros((rows, LANES), F32)
        stack = jnp.concatenate(
            [keys * (lane_head == i).astype(F32).astype(BF16) for i in range(per)], axis=0
        )
        scores = dot_nt(stack, q)
        for i in range(per):
            here = lane_head == i
            s = scores[i * rows : (i + 1) * rows, :] * scale + dead
            top = jnp.max(s, axis=0, keepdims=True)
            p = jnp.exp2(s - top).astype(BF16)
            p_ref[group * per + i] = p
            both = dot_tn(p, values)
            rinv = 1.0 / both[:, LANES:]
            acc = jnp.where(here, both[:, :LANES] * rinv, acc)
            racc = jnp.where(here, rinv, racc)
        o_ref[:, at : at + LANES] = acc.astype(BF16)
        rinv_ref[:, at : at + LANES] = racc
    waits[0]()
    x2 = x + (dot(o_ref[...], w_out[...]) + vector(vecs, B_OUT))
    x2_ref[...] = x2
    xhat2, _ = norm_stats(x2)
    n2 = (xhat2 * vector(vecs, GAIN2) + vector(vecs, BIAS2)).astype(BF16)
    n2_ref[...] = n2
    hidden = w_up.shape[1]
    step = width
    waits[1]()
    for start in range(0, hidden, step):
        cols = slice(start, start + step)
        u = dot(n2, w_up[:, cols]) + vector(vecs, B_UP + start // step)
        cdf = 0.5 + 0.5 * lax.erf(u * (0.5**0.5))
        pdf = jnp.exp(-0.5 * u * u) * 0.3989422804014327
        h_ref[:, cols] = (u * cdf).astype(BF16)
        gp_ref[:, cols] = (cdf + u * pdf).astype(BF16)
    waits[2]()


def down_kernel(depth, order, down, count, share, *refs):
    cs, (vecs, h_ref, g_ref, keep_ref, send_ref) = refs[:count], refs[count:]
    core, place, _ = place_of()
    quota = vecs[QUOTA : QUOTA + 1, 0:1].astype(jnp.int32)
    live_rows = lax.broadcasted_iota(jnp.int32, (share, 1), 0) < quota
    for k in range(count):
        g_ref[k * share : (k + 1) * share, :] = jnp.where(
            live_rows, cs[k][:share, :].astype(F32), 0.0
        ).astype(BF16)
    weight_grad(keep_ref, send_ref, core, place, depth, order, down, 0, h_ref, g_ref)


def middle_kernel(
    depth,
    order,
    up,
    after,
    g_ref, gp_ref, h_ref, n2_ref, o_ref, x2_ref, vecs, w_up, w_down,
    keep_ref, send_ref, dx2_ref, dx2r_ref, out_ref, small_ref, du_ref,
):
    core, place, _ = place_of()
    g = g_ref[...]
    hidden = w_up.shape[1]
    width = g.shape[1]
    step = 512
    small_ref[...] = jnp.zeros(small_ref.shape, F32)
    dn2 = jnp.zeros((g.shape[0], width), F32)
    for start in range(0, hidden, step):
        cols = slice(start, start + step)
        dh = dot_nt(g, w_down[cols, :])
        du = (dh * gp_ref[:, cols].astype(F32)).astype(BF16)
        du_ref[:, cols] = du
        small_ref[0:1, cols] = jnp.sum(du.astype(F32), axis=0, keepdims=True)
        dn2 = dn2 + dot_nt(du, w_up[:, cols])
    x2 = x2_ref[...]
    xhat, rstd = norm_stats(x2)
    gf = g.astype(F32)
    dx2 = gf + norm_back(dn2, xhat, rstd, vector(vecs, GAIN2))
    dx2_ref[...] = dx2
    dx2r = dx2.astype(BF16)
    dx2r_ref[...] = dx2r
    small_ref[1:2, 0:width] = jnp.sum(dx2r.astype(F32), axis=0, keepdims=True)
    small_ref[1:2, width : 2 * width] = jnp.sum(dn2 * xhat, axis=0, keepdims=True)
    small_ref[1:2, 2 * width : 3 * width] = jnp.sum(dn2, axis=0, keepdims=True)
    small_ref[1:2, 3 * width : 4 * width] = jnp.sum(gf, axis=0, keepdims=True)
    weight_grad(keep_ref, send_ref, core, place, depth, order, up, 0, n2_ref, du_ref)
    weight_grad(keep_ref, send_ref, core, place, depth, order, after, up.tall, o_ref, dx2r_ref)
    out_ref[...] = (x2 + (dot(h_ref[...], w_down[...]) + vector(vecs, B_DOWN))).astype(BF16)


def backward_kernel(
    depth,
    order,
    proj,
    count,
    share,
    *refs,
):
    refs = list(refs)
    xs = [refs.pop(0) for _ in range(count)]
    cs = [refs.pop(0) for _ in range(count)]
    qkv_ref, p_ref, rinv_ref, o_ref, dx2_ref, dx2r_ref, block_ref, sub_ref, vecs, w_qkv, w_out = refs[:11]
    refs = refs[11:]
    results = [refs.pop(0) for _ in range(3)]
    keep_ref, send_ref, dqkv_ref, small = refs
    core, place, _ = place_of()
    rows = count * share
    width = xs[0].shape[1]
    head = width // HEADS
    per = LANES // head
    d_o = dot_nt(dx2r_ref[...], w_out[...]).astype(BF16).astype(F32)
    d_scaled = d_o * rinv_ref[...]
    product = (d_scaled * o_ref[...].astype(F32)).astype(BF16)
    d_scaled = d_scaled.astype(BF16)
    lane_head = lax.broadcasted_iota(jnp.int32, (1, LANES), 1) // head
    minus = jnp.full((rows, LANES), -1.0, BF16)
    scale = head ** (-0.5)
    for group in range(width // LANES):
        at = group * LANES
        q = qkv_ref[:, at : at + LANES]
        keys = qkv_ref[:, width + at : width + at + LANES]
        values = qkv_ref[:, 2 * width + at : 2 * width + at + LANES]
        ds_o = d_scaled[:, at : at + LANES]
        rhs = jnp.concatenate([ds_o, product[:, at : at + LANES]], axis=1)
        dq = jnp.zeros((rows, LANES), F32)
        dk = jnp.zeros((rows, LANES), F32)
        dv = jnp.zeros((rows, LANES), F32)
        stack = jnp.concatenate(
            [
                jnp.concatenate(
                    [
                        values * (lane_head == i).astype(F32).astype(BF16),
                        minus * (lane_head == i).astype(F32).astype(BF16),
                    ],
                    axis=1,
                )
                for i in range(per)
            ],
            axis=0,
        )
        p = p_ref[group * per : (group + 1) * per].reshape(per * rows, rows)
        ds = (p.astype(F32) * dot_nt(stack, rhs)).astype(BF16)
        dks = dot(ds, q)
        dvs = dot(p, ds_o)
        for i in range(per):
            here = lane_head == i
            part = slice(i * rows, (i + 1) * rows)
            dq = jnp.where(here, dot_tn(ds[part, :], keys), dq)
            dk = jnp.where(here, dks[part, :], dk)
            dv = jnp.where(here, dvs[part, :], dv)
        dqkv_ref[:, at : at + LANES] = (dq * scale).astype(BF16)
        dqkv_ref[:, width + at : width + at + LANES] = (dk * scale).astype(BF16)
        dqkv_ref[:, 2 * width + at : 2 * width + at + LANES] = dv.astype(BF16)
    x = jnp.concatenate([ref[...] for ref in xs], axis=0).astype(F32)
    xhat, rstd = norm_stats(x)
    gain = vector(vecs, GAIN1)
    n1 = (xhat * gain + vector(vecs, BIAS1)).astype(BF16)
    weight_grad(keep_ref, send_ref, core, place, depth, order, proj, 0, n1, dqkv_ref)
    dn1 = dot_nt(dqkv_ref[...], w_qkv[...])
    dx = (dx2_ref[...] + norm_back(dn1, xhat, rstd, gain)).astype(BF16)
    d_mask = jnp.zeros((16, width), F32)
    for k in range(count):
        part = dx[k * share : (k + 1) * share, :]
        d_mask = d_mask + dot(cs[k][share : share + 16, :share], part)
        ref, at = results[min(k, 2)], 2 * share * max(k - 2, 0)
        ref[at : at + share, :] = block_ref[k * share : (k + 1) * share, :]
        ref[at + share : at + 2 * share, :] = part
    blocks = small.shape[0]
    small[...] = jnp.zeros(small.shape, F32)
    wide = [
        d_mask[0:1, :],
        jnp.sum(dn1 * xhat, axis=0, keepdims=True),
        jnp.sum(dn1, axis=0, keepdims=True),
        jnp.sum(dqkv_ref[:, :width].astype(F32), axis=0, keepdims=True),
        jnp.sum(dqkv_ref[:, 2 * width :].astype(F32), axis=0, keepdims=True),
        sub_ref[1:2, :],
        sub_ref[0:1, :],
    ]
    lines = [v[:, j : j + LANES] for v in wide for j in range(0, v.shape[1], LANES)]
    each = -(-len(lines) // blocks)
    for i, line in enumerate(lines):
        small[i // each, i % each : i % each + 1, :] = line
    chips = blocks // 2
    for out_ref, owner in ((send_ref, core ^ 1), (keep_ref, core)):
        for index in range(chips):
            rel = relative(owner, place, chip_of(index, depth), depth, order)
            out_ref[rel, proj.tall : proj.tall + 16, :] = small[owner * chips + index].astype(BF16)


def gather_kernel(depth, order, layout, scale, small_at, sizes, *refs):
    count = len(layout)
    halves, outs = refs[:4], refs[4 : 4 + count]
    vectors = refs[4 + count : 4 + count + len(sizes)]
    held = refs[4 + count + len(sizes) : -2]
    small, sems = refs[-2:]
    core, place, _ = place_of()
    half = halves[0].shape[0]
    chips = 2 * half
    copies = []
    for side, owner in ((0, core), (1, core ^ 1)):
        for rel in range(chips):
            ref, at_block = halves[2 * side + rel // half], rel % half
            index = absolute(owner, place, rel, depth, order)
            slot = side * chips + rel
            for which, (pieces, base) in enumerate(layout):
                for j in range(pieces.width // LANES):
                    at = base + j * pieces.height
                    held[which][slot, :, j * LANES : (j + 1) * LANES] = (
                        ref[at_block, at : at + pieces.height, :].astype(F32) * scale
                    )
                top = pl.multiple_of((index // pieces.lane_blocks) * pieces.height, 16)
                lane = owner * pieces.half + (index % pieces.lane_blocks) * pieces.width
                copy = pltpu.make_async_copy(
                    held[which].at[slot],
                    outs[which].at[
                        pl.ds(top, pieces.height),
                        pl.ds(pl.multiple_of(lane, LANES), pieces.width),
                    ],
                    sems.at[which, slot],
                )
                copy.start()
                copies.append(copy)
            if sizes:
                small[owner * chips + index] = (
                    ref[at_block, small_at : small_at + 16, :].astype(F32) * scale
                )
    lines = sum(sizes) // LANES
    each = max(1, -(-lines // (2 * chips)))
    line = 0
    for out, size in zip(vectors, sizes):
        for j in range(size // LANES):
            out[j * LANES : (j + 1) * LANES] = small[
                line // each, line % each : line % each + 1, :
            ].reshape(LANES)
            line += 1
    for copy in copies:
        copy.wait()


def finish_kernel(flags, *refs):
    block_out, token_grad = refs[-2:]
    share = block_out.shape[1]
    blk = lax.axis_index("blk")
    for k, ref in enumerate(refs[:-2]):
        at = blk ^ k
        block_out[at] = ref[:share, :]
        token_grad[at] = jnp.where(
            flag_column(flags, at), 0.0, ref[share : 2 * share, :].astype(F32)
        )


WHOLE = pl.BlockSpec(memory_space=pltpu.VMEM)
FAR = pl.BlockSpec(memory_space=pltpu.HBM)


def call(kernel, outs, *args, scratch=(), far=0, far_outs=0, name=None):
    args = list(args)
    for i in range(far):
        args[i] = pltpu.with_memory_space_constraint(args[i], pltpu.HBM)
    return pl.pallas_call(
        kernel,
        out_shape=tuple(outs),
        in_specs=[FAR] * far + [WHOLE] * (len(args) - far),
        out_specs=tuple([FAR] * far_outs + [WHOLE] * (len(outs) - far_outs)),
        scratch_shapes=list(scratch),
        compiler_params=pltpu.CompilerParams(vmem_limit_bytes=VMEM_LIMIT),
        cost_estimate=pl.CostEstimate(
            flops=int(US.get(name, 0) * 1.15e9), bytes_accessed=0, transcendentals=0
        ),
        name=name,
    )(*args)


def like(array):
    return pltpu.VMEM(array.shape, array.dtype)


def after(value, *others):
    return lax.optimization_barrier((value, *others))[0]


def shape(dims, kind=BF16):
    return jax.ShapeDtypeStruct(tuple(dims), kind)


def add(*parts):
    total = parts[0].astype(F32)
    for part in parts[1:]:
        total = total + part.astype(F32)
    return total.astype(BF16)


def shards(
    dp_size,
    blk_size,
    tokens,
    mask_flags,
    buckets,
    cotangent,
    mask_token,
    norm1_gain,
    norm1_bias,
    w_qkv,
    b_query,
    b_value,
    w_out,
    b_out,
    norm2_gain,
    norm2_bias,
    w_up,
    b_up,
    w_down,
    b_down,
):
    micro_count, images, share, width = tokens.shape
    hidden = w_up.shape[1]
    count = micro_count * images
    rows = count * share
    deep = dp_size // 2
    depth = deep // 2
    chips = 4 * depth
    total_images = float(micro_count * images * dp_size)

    def send(value, change):
        table = []
        for d in range(dp_size):
            for b in range(blk_size):
                nz, ny, nx, nc = change(d // 2, d % 2, b // 2, b % 2)
                table.append((d * blk_size + b, (nz * 2 + ny) * blk_size + nx * 2 + nc))
        return lax.ppermute(value, ("dp", "blk"), table)

    def core_pair(z, y, x, c):
        return z, y, x, c ^ 1

    def depth_pair(k):
        return lambda z, y, x, c: (z ^ k, y, x, c)

    def image_pair(k):
        return lambda z, y, x, c: (z, y, x ^ (k >> 1), c ^ (k & 1))

    def halving(order):
        def flip(bits):
            def change(z, y, x, c):
                axis, bit = bits[c]
                at = {"z": z, "y": y, "x": x}
                at[axis] ^= bit
                return at["z"], at["y"], at["x"], c

            return change

        return [flip(bits) for bits in zip(*exchanges(order, depth))]

    class Sum:
        def __init__(self, keep, sent, order):
            self.order = order
            self.pairs = halving(order)
            self.keep, self.sent = keep, sent
            self.step = 0

        def cores(self, *behind):
            self.got = send(after(self.sent, *behind) if behind else self.sent, core_pair)
            return self

        def advance(self, *behind):
            count = len(self.pairs)
            if self.step < count:
                half = self.keep.shape[0] // 2
                away = add(self.keep[half:], self.got[half:])
                self.keep = add(self.keep[:half], self.got[:half])
                change = self.pairs[self.step]
            elif self.step == count:
                away = self.keep = add(self.keep, self.got)
                change = depth_pair(depth)
            else:
                if self.step == count + 1:
                    self.keep = add(self.keep, self.got)
                else:
                    self.keep = jnp.concatenate([self.keep, self.got])
                away = self.keep
                change = self.pairs[2 * count - self.step]
            self.got = send(after(away, *behind) if behind else away, change)
            self.step += 1

        @property
        def left(self):
            return 2 * len(self.pairs) + 1 - self.step

        def finish(self):
            mine = (self.keep, self.got)
            return mine + tuple(send(a, core_pair) for a in mine)

    down = Pieces(hidden, width, chips)
    up = Pieces(width, hidden, chips)
    out = Pieces(width, width, chips)
    proj = Pieces(width, 3 * width, chips)
    dma = pltpu.SemaphoreType.DMA

    tokens_in = tokens.reshape(count, share, width)
    flags = mask_flags.reshape(count, 1, share)
    cots_in = cotangent.reshape(count, share, width)
    filled = call(
        functools.partial(fill_kernel, count),
        [shape((share, width))] * count + [shape((share + 16, width))] * count,
        tokens_in,
        cots_in,
        flags,
        mask_token,
        far=4,
        scratch=[like(tokens_in), like(cots_in), like(flags), like(mask_token), dma((4,))],
        name="fill",
    )
    xs = list(filled[:1]) + [send(filled[k], image_pair(k)) for k in range(1, count)]
    cs = [filled[count]] + [
        send(after(filled[count + k], xs[1]), image_pair(k)) for k in range(1, count)
    ]
    vectors = [norm1_gain, norm1_bias, b_query, b_value, b_out, norm2_gain, norm2_bias, b_down, b_up]
    w_qkv, vecs = call(
        functools.partial(prefetch_kernel, images),
        [shape(w_qkv.shape), shape((16, width), F32)],
        after(w_qkv, xs[1]),
        buckets.T,
        *vectors,
        far=2 + len(vectors),
        scratch=[like(v) for v in vectors] + [like(buckets.T), dma((2 + len(vectors),))],
        name="prefetch",
    )
    weights = [w_out, w_up, w_down]
    w_out, w_up, w_down, qkv, p, rinv, o, x2, n2, h, gp = call(
        functools.partial(forward_kernel, count, share),
        [shape(w.shape) for w in weights]
        + [
            shape((rows, 3 * width)),
            shape((HEADS, rows, rows)),
            shape((rows, width), F32),
            shape((rows, width)),
            shape((rows, width), F32),
            shape((rows, width)),
            shape((rows, hidden)),
            shape((rows, hidden)),
        ],
        *weights,
        *xs,
        vecs,
        w_qkv,
        far=len(weights),
        scratch=[dma((len(weights),))],
        name="forward",
    )
    g, keep, sent = call(
        functools.partial(down_kernel, depth, ORDERS[0], down, count, share),
        [shape((rows, width))] + [shape((chips, down.tall, LANES))] * 2,
        *cs,
        vecs,
        h,
        name="down",
    )
    one = Sum(keep, sent, ORDERS[0]).cores()
    keep, sent, dx2, dx2r, block, sub = call(
        functools.partial(middle_kernel, depth, ORDERS[1], up, out),
        [shape((chips, up.tall + out.tall, LANES))] * 2
        + [
            shape((rows, width), F32),
            shape((rows, width)),
            shape((rows, width)),
            shape((8, hidden), F32),
        ],
        g,
        gp,
        h,
        n2,
        o,
        x2,
        vecs,
        w_up,
        w_down,
        scratch=[pltpu.VMEM((rows, hidden), BF16)],
        name="middle",
    )
    two = Sum(keep, sent, ORDERS[1]).cores()
    early = [one.got, two.got][:BEFORE]
    if early:
        dx2r = after(dx2r, *early)
    one.advance()
    *results, keep, sent = call(
        functools.partial(backward_kernel, depth, ORDERS[2], proj, count, share),
        [shape((2 * share, width))] * 2
        + [shape((2 * share * (count - 2), width))]
        + [shape((chips, proj.tall + 16, LANES))] * 2,
        *xs,
        *cs,
        qkv,
        p,
        rinv,
        o,
        dx2,
        dx2r,
        block,
        sub,
        vecs,
        w_qkv,
        w_out,
        scratch=[
            pltpu.VMEM((rows, 3 * width), BF16),
            pltpu.VMEM((2 * chips, 16, LANES), F32),
        ],
        name="backward",
    )
    three = Sum(keep, sent, ORDERS[2])
    three.cores(*[two.got][:THIRD])
    def whole(group, layout, small_at=0, sizes=(), name=None):
        outs = [shape((p.rows, 2 * p.half), F32) for p, _ in layout]
        outs += [shape((n,), F32) for n in sizes]
        return call(
            functools.partial(
                gather_kernel, depth, group.order, layout, 1.0 / total_images, small_at, sizes
            ),
            outs,
            *group.finish(),
            far_outs=len(layout),
            scratch=[pltpu.VMEM((2 * chips, p.height, p.width), F32) for p, _ in layout]
            + [pltpu.VMEM((2 * chips, 16, LANES), F32), dma((len(layout), 2 * chips))],
            name=name,
        )

    groups = (one, two, three)
    layouts = ([(down, 0)], [(up, 0), (out, up.tall)], [(proj, 0)])
    names = ("gather_down", "gather_up", "gather_proj")
    sizes = (width,) * 9 + (hidden,)
    done = {(3, 0): keep, (0, 0): one.got}
    grads = {}
    progress = True
    while progress:
        progress = False
        for which in (2, 1, 0):
            group = groups[which]
            if which in grads:
                continue
            waits = [b for a, b in TIES if a == (which, group.step)]
            waits += [(4, b) for a, b in WRITTEN if a == (which, group.step)]
            if any(w not in done for w in waits):
                continue
            progress = True
            behind = [done[w] for w in waits]
            if group.left:
                group.advance(*behind)
                done[which, group.step - 1] = group.got
            else:
                if behind:
                    group.got = after(group.got, *behind)
                grads[which] = whole(
                    group,
                    layouts[which],
                    proj.tall if which == 2 else 0,
                    sizes if which == 2 else (),
                    name=names[which],
                )
                done[4, which] = grads[which][0]
        if (5, 0) not in done and RESULTS in done:
            own, near, far = results
            far = send(after(far, done[RESULTS]), image_pair(2))
            near = send(after(near, done[RESULTS]), image_pair(1))
            results = [own, near, far, send(far[2 * share :], image_pair(1))]
            done[5, 0] = results[-1]
            progress = True
    (grad_down,), (grad_up, grad_out), (grad_proj, *small) = (grads[i] for i in range(3))
    mask_g, gain1_g, bias1_g, query_g, value_g, after_g, gain2_g, bias2_g, reduce_g, expand_g = small

    block_out, token_grad = call(
        finish_kernel,
        [shape((count, share, width)), shape((count, share, width), F32)],
        flags,
        *results,
        name="finish",
    )
    return (
        block_out.reshape(tokens.shape),
        token_grad.reshape(tokens.shape),
        mask_g,
        gain1_g,
        bias1_g,
        grad_proj,
        query_g,
        value_g,
        grad_out,
        after_g,
        gain2_g,
        bias2_g,
        grad_up,
        expand_g,
        grad_down,
        reduce_g,
    )


def solution(mesh):
    rows = P(None, "dp", "blk", None)
    placed = (rows, P(None, "dp", "blk"), P(None, "dp"), rows) + (P(),) * 14
    return jax.shard_map(
        functools.partial(shards, mesh.shape["dp"], mesh.shape["blk"]),
        mesh=mesh,
        in_specs=placed,
        out_specs=(rows, rows) + (P(),) * 14,
        check_vma=False,
    )
```

```python
import functools

import jax
import jax.numpy as jnp
from jax import lax
from jax.experimental import pallas as pl
from jax.experimental.pallas import tpu as pltpu
from jax.sharding import PartitionSpec as P

HEADS = 16
LANES = 128
EPS = 1e-06
LOG2E = 1.4426950408889634
BF16 = jnp.bfloat16
F32 = jnp.float32
ORDERS = (('zxy', 'yxz'), ('yzx', 'zxy'), ('yzx', 'xzy'))
TIES = (((2, 2), (5, 0)), ((0, 2), (1, 0)), ((1, 3), (0, 1)), ((0, 1), (3, 0)), ((2, 4), (1, 4)), ((0, 6), (1, 5)), ((2, 5), (1, 2)), ((2, 1), (3, 0)), ((2, 2), (0, 1)), ((0, 2), (3, 0)), ((2, 3), (1, 2)), ((1, 0), (3, 0)), ((2, 5), (7, 0)))
RESULTS = (1, 2)
WRITTEN = ()
BEFORE = 1
THIRD = 1
US = {'forward': 15, 'gather_up': 8}
VMEM_LIMIT = 24 * 1024 * 1024


def dot(a, b):
    return jnp.dot(a, b, preferred_element_type=F32)


def dot_nt(a, b):
    return lax.dot_general(a, b, (((1,), (1,)), ((), ())), preferred_element_type=F32)


def dot_tn(a, b):
    return lax.dot_general(a, b, (((0,), (0,)), ((), ())), preferred_element_type=F32)


def row(ref):
    return ref[...].astype(F32).reshape(1, -1)


def norm_stats(rows):
    centre = jnp.mean(rows, axis=-1, keepdims=True)
    centred = rows - centre
    spread = jnp.mean(centred * centred, axis=-1, keepdims=True)
    rstd = lax.rsqrt(spread + EPS)
    return centred * rstd, rstd


def norm_back(grad_normed, xhat, rstd, gain):
    grad_xhat = grad_normed * gain
    first = jnp.mean(grad_xhat, axis=-1, keepdims=True)
    second = jnp.mean(grad_xhat * xhat, axis=-1, keepdims=True)
    return rstd * (grad_xhat - first - xhat * second)


class Pieces:
    def __init__(self, rows, cols, chips):
        self.rows = rows
        self.half = cols // 2
        self.row_blocks = min(chips, rows // 16)
        self.lane_blocks = chips // self.row_blocks
        self.height = rows // self.row_blocks
        self.width = self.half // self.lane_blocks
        self.tall = self.height * self.width // LANES


def exchanges(order, depth):
    deep = [("z", 1 << i) for i in reversed(range(depth.bit_length() - 1))]
    bits = {"x": [("x", 1)], "y": [("y", 1)], "z": deep}
    return [sum((bits[axis] for axis in axes), []) for axes in order]


def relative(core, place, chip, depth, order):
    differ = dict(zip("xyz", (a ^ b for a, b in zip(place, chip))))
    found = []
    for bits in exchanges(order, depth):
        at = 0
        for axis, bit in bits:
            at = at * 2 + ((differ[axis] & bit) // bit)
        found.append(at)
    return jnp.where(core == 0, *found)


def chip_of(index, depth):
    return index // (2 * depth), (index // depth) % 2, index % depth


def absolute(core, place, index, depth, order):
    flips = []
    for bits in exchanges(order, depth):
        flip = dict.fromkeys("xyz", 0)
        for i, (axis, bit) in enumerate(reversed(bits)):
            flip[axis] |= bit * ((index >> i) & 1)
        flips.append(flip)
    x, y, z = (
        at ^ jnp.where(core == 0, flips[0][axis], flips[1][axis]) for axis, at in zip("xyz", place)
    )
    return (x * 2 + y) * depth + z % depth


def store_pieces(out_ref, core, place, depth, order, pieces, base, value, row_start):
    for first in range(0, value.shape[0], pieces.height):
        row_block = (row_start + first) // pieces.height
        for lane_block in range(pieces.lane_blocks):
            index = row_block * pieces.lane_blocks + lane_block
            rel = relative(core, place, chip_of(index, depth), depth, order)
            for j in range(pieces.width // LANES):
                at = base + j * pieces.height
                lane = lane_block * pieces.width + j * LANES
                out_ref[rel, at : at + pieces.height, :] = value[
                    first : first + pieces.height, lane : lane + LANES
                ].astype(BF16)


def weight_grad(keep_ref, send_ref, core, place, depth, order, pieces, base, lhs, rhs_ref):
    stripe = max(pieces.height, min(512, pieces.rows))
    for out_ref, owner in ((send_ref, core ^ 1), (keep_ref, core)):
        rhs = rhs_ref[:, pl.ds(pl.multiple_of(owner * pieces.half, LANES), pieces.half)]
        for start in range(0, pieces.rows, stripe):
            value = dot_tn(lhs[:, start : start + stripe], rhs)
            store_pieces(out_ref, owner, place, depth, order, pieces, base, value, start)


def place_of():
    dp, blk = lax.axis_index("dp"), lax.axis_index("blk")
    return blk % 2, (blk // 2, dp % 2, dp // 2), blk


def fetch(sems, *pairs):
    copies = [pltpu.make_async_copy(a, b, sems.at[i]) for i, (a, b) in enumerate(pairs)]
    for copy in copies:
        copy.start()
    return [copy.wait for copy in copies]


def flag_column(flags, at):
    share = flags.shape[2]
    eye = lax.broadcasted_iota(jnp.int32, (share, share), 0) == lax.broadcasted_iota(
        jnp.int32, (share, share), 1
    )
    return jnp.sum(jnp.where(eye, flags[at], 0), axis=1, keepdims=True) == 1


def fill_kernel(count, tokens_hbm, cotangent_hbm, flags_hbm, mask_hbm, *refs):
    outs, cots = refs[:count], refs[count : 2 * count]
    tokens, cotangent, flags, mask_token, sems = refs[2 * count :]
    waits = fetch(
        sems,
        (tokens_hbm, tokens),
        (flags_hbm, flags),
        (mask_hbm, mask_token),
        (cotangent_hbm, cotangent),
    )
    for wait in waits[:3]:
        wait()
    blk = lax.axis_index("blk")
    share = tokens.shape[1]
    for k in range(count):
        at = blk ^ k
        outs[k][...] = jnp.where(
            flag_column(flags, at), row(mask_token), tokens[at].astype(F32)
        ).astype(BF16)
    waits[3]()
    for k in range(count):
        at = blk ^ k
        cots[k][:share, :] = cotangent[at]
        cots[k][share:, :] = jnp.zeros((16, cots[k].shape[1]), BF16)
        first = lax.broadcasted_iota(jnp.int32, (16, share), 0) == 0
        flag = (flags[at] == 1).astype(F32)
        cots[k][share:, :share] = jnp.where(first, flag, 0.0).astype(BF16)


GAIN1, BIAS1, B_QUERY, B_VALUE, B_OUT, GAIN2, BIAS2, B_DOWN, B_UP = range(9)
QUOTA = 15


def prefetch_kernel(images, weight_hbm, buckets_hbm, *refs):
    count = (len(refs) - 4) // 2
    weight, vecs = refs[count : count + 2]
    held, buckets, sems = refs[count + 2 : -2], refs[-2], refs[-1]
    waits = fetch(
        sems, (weight_hbm, weight), (buckets_hbm, buckets), *zip(refs[:count], held)
    )
    for wait in waits[1:]:
        wait()
    width = vecs.shape[1]
    vecs[...] = jnp.zeros(vecs.shape, F32)
    line = 0
    for ref in held:
        for at in range(0, ref.shape[0], width):
            vecs[line : line + 1, :] = row(ref)[:, at : at + width]
            line += 1
    micro = lax.axis_index("blk") // images
    quota = jnp.zeros((1, 1), jnp.int32)
    for m in range(buckets.shape[1]):
        bucket = buckets[:, m : m + 1]
        here = jnp.where(bucket == 0, 25, jnp.where(bucket == 1, 49, 64))
        quota = quota + jnp.where(micro == m, here, 0)
    vecs[QUOTA : QUOTA + 1, :] = jnp.broadcast_to(quota.astype(F32), (1, width))
    waits[0]()


def vector(rows, which):
    return rows[which : which + 1, :]


def forward_kernel(count, share, *refs):
    sources, refs = refs[:3], refs[3:]
    xs, refs = refs[:count], refs[count:]
    vecs, w_qkv = refs[:2]
    targets = refs[2:5]
    qkv_ref, p_ref, rinv_ref, o_ref, x2_ref, n2_ref, h_ref, gp_ref, sems = refs[5:]
    waits = fetch(sems, *zip(sources, targets))
    w_out, w_up, _ = targets
    quota = vecs[QUOTA : QUOTA + 1, 0:1].astype(jnp.int32)
    width = xs[0].shape[1]
    head = width // HEADS
    rows = count * share
    x = jnp.concatenate([ref[...] for ref in xs], axis=0).astype(F32)
    xhat, _ = norm_stats(x)
    n1 = (xhat * vector(vecs, GAIN1) + vector(vecs, BIAS1)).astype(BF16)
    for part in range(3):
        cols = slice(part * width, (part + 1) * width)
        value = dot(n1, w_qkv[:, cols])
        if part == 0:
            value = value + vector(vecs, B_QUERY)
        if part == 2:
            value = value + vector(vecs, B_VALUE)
        qkv_ref[:, cols] = value.astype(BF16)
    key = lax.broadcasted_iota(jnp.int32, (rows, 1), 0)
    dead = jnp.where(key % share < quota, 0.0, -1e30).astype(F32)
    lane_head = lax.broadcasted_iota(jnp.int32, (1, LANES), 1) // head
    scale = head ** (-0.5) * LOG2E
    per = LANES // head
    ones = jnp.ones((rows, LANES), BF16)
    for group in range(width // LANES):
        at = group * LANES
        q = qkv_ref[:, at : at + LANES]
        keys = qkv_ref[:, width + at : width + at + LANES]
        values = jnp.concatenate(
            [qkv_ref[:, 2 * width + at : 2 * width + at + LANES], ones], axis=1
        )
        acc = jnp.zeros((rows, LANES), F32)
        racc = jnp.zeros((rows, LANES), F32)
        stack = jnp.concatenate(
            [keys * (lane_head == i).astype(F32).astype(BF16) for i in range(per)], axis=0
        )
        scores = dot_nt(stack, q)
        for i in range(per):
            here = lane_head == i
            s = scores[i * rows : (i + 1) * rows, :] * scale + dead
            top = jnp.max(s, axis=0, keepdims=True)
            p = jnp.exp2(s - top).astype(BF16)
            p_ref[group * per + i] = p
            both = dot_tn(p, values)
            rinv = 1.0 / both[:, LANES:]
            acc = jnp.where(here, both[:, :LANES] * rinv, acc)
            racc = jnp.where(here, rinv, racc)
        o_ref[:, at : at + LANES] = acc.astype(BF16)
        rinv_ref[:, at : at + LANES] = racc
    waits[0]()
    x2 = x + (dot(o_ref[...], w_out[...]) + vector(vecs, B_OUT))
    x2_ref[...] = x2
    xhat2, _ = norm_stats(x2)
    n2 = (xhat2 * vector(vecs, GAIN2) + vector(vecs, BIAS2)).astype(BF16)
    n2_ref[...] = n2
    hidden = w_up.shape[1]
    step = width
    waits[1]()
    for start in range(0, hidden, step):
        cols = slice(start, start + step)
        u = dot(n2, w_up[:, cols]) + vector(vecs, B_UP + start // step)
        cdf = 0.5 + 0.5 * lax.erf(u * (0.5**0.5))
        pdf = jnp.exp(-0.5 * u * u) * 0.3989422804014327
        h_ref[:, cols] = (u * cdf).astype(BF16)
        gp_ref[:, cols] = (cdf + u * pdf).astype(BF16)
    waits[2]()


def down_kernel(depth, order, down, count, share, *refs):
    cs, (vecs, h_ref, g_ref, keep_ref, send_ref) = refs[:count], refs[count:]
    core, place, _ = place_of()
    quota = vecs[QUOTA : QUOTA + 1, 0:1].astype(jnp.int32)
    live_rows = lax.broadcasted_iota(jnp.int32, (share, 1), 0) < quota
    for k in range(count):
        g_ref[k * share : (k + 1) * share, :] = jnp.where(
            live_rows, cs[k][:share, :].astype(F32), 0.0
        ).astype(BF16)
    weight_grad(keep_ref, send_ref, core, place, depth, order, down, 0, h_ref, g_ref)


def middle_kernel(
    depth,
    order,
    up,
    after,
    g_ref, gp_ref, h_ref, n2_ref, o_ref, x2_ref, vecs, w_up, w_down,
    keep_ref, send_ref, dx2_ref, dx2r_ref, out_ref, small_ref, du_ref,
):
    core, place, _ = place_of()
    g = g_ref[...]
    hidden = w_up.shape[1]
    width = g.shape[1]
    step = 512
    small_ref[...] = jnp.zeros(small_ref.shape, F32)
    dn2 = jnp.zeros((g.shape[0], width), F32)
    for start in range(0, hidden, step):
        cols = slice(start, start + step)
        dh = dot_nt(g, w_down[cols, :])
        du = (dh * gp_ref[:, cols].astype(F32)).astype(BF16)
        du_ref[:, cols] = du
        small_ref[0:1, cols] = jnp.sum(du.astype(F32), axis=0, keepdims=True)
        dn2 = dn2 + dot_nt(du, w_up[:, cols])
    x2 = x2_ref[...]
    xhat, rstd = norm_stats(x2)
    gf = g.astype(F32)
    dx2 = gf + norm_back(dn2, xhat, rstd, vector(vecs, GAIN2))
    dx2_ref[...] = dx2
    dx2r = dx2.astype(BF16)
    dx2r_ref[...] = dx2r
    small_ref[1:2, 0:width] = jnp.sum(dx2r.astype(F32), axis=0, keepdims=True)
    small_ref[1:2, width : 2 * width] = jnp.sum(dn2 * xhat, axis=0, keepdims=True)
    small_ref[1:2, 2 * width : 3 * width] = jnp.sum(dn2, axis=0, keepdims=True)
    small_ref[1:2, 3 * width : 4 * width] = jnp.sum(gf, axis=0, keepdims=True)
    weight_grad(keep_ref, send_ref, core, place, depth, order, up, 0, n2_ref, du_ref)
    weight_grad(keep_ref, send_ref, core, place, depth, order, after, up.tall, o_ref, dx2r_ref)
    out_ref[...] = (x2 + (dot(h_ref[...], w_down[...]) + vector(vecs, B_DOWN))).astype(BF16)


def backward_kernel(
    depth,
    order,
    proj,
    count,
    share,
    *refs,
):
    refs = list(refs)
    xs = [refs.pop(0) for _ in range(count)]
    cs = [refs.pop(0) for _ in range(count)]
    qkv_ref, p_ref, rinv_ref, o_ref, dx2_ref, dx2r_ref, block_ref, sub_ref, vecs, w_qkv, w_out = refs[:11]
    refs = refs[11:]
    results = [refs.pop(0) for _ in range(3)]
    keep_ref, send_ref, dqkv_ref, small = refs
    core, place, _ = place_of()
    rows = count * share
    width = xs[0].shape[1]
    head = width // HEADS
    per = LANES // head
    d_o = dot_nt(dx2r_ref[...], w_out[...]).astype(BF16).astype(F32)
    d_scaled = d_o * rinv_ref[...]
    product = (d_scaled * o_ref[...].astype(F32)).astype(BF16)
    d_scaled = d_scaled.astype(BF16)
    lane_head = lax.broadcasted_iota(jnp.int32, (1, LANES), 1) // head
    minus = jnp.full((rows, LANES), -1.0, BF16)
    scale = head ** (-0.5)
    for group in range(width // LANES):
        at = group * LANES
        q = qkv_ref[:, at : at + LANES]
        keys = qkv_ref[:, width + at : width + at + LANES]
        values = qkv_ref[:, 2 * width + at : 2 * width + at + LANES]
        ds_o = d_scaled[:, at : at + LANES]
        rhs = jnp.concatenate([ds_o, product[:, at : at + LANES]], axis=1)
        dq = jnp.zeros((rows, LANES), F32)
        dk = jnp.zeros((rows, LANES), F32)
        dv = jnp.zeros((rows, LANES), F32)
        stack = jnp.concatenate(
            [
                jnp.concatenate(
                    [
                        values * (lane_head == i).astype(F32).astype(BF16),
                        minus * (lane_head == i).astype(F32).astype(BF16),
                    ],
                    axis=1,
                )
                for i in range(per)
            ],
            axis=0,
        )
        p = p_ref[group * per : (group + 1) * per].reshape(per * rows, rows)
        ds = (p.astype(F32) * dot_nt(stack, rhs)).astype(BF16)
        dks = dot(ds, q)
        dvs = dot(p, ds_o)
        for i in range(per):
            here = lane_head == i
            part = slice(i * rows, (i + 1) * rows)
            dq = jnp.where(here, dot_tn(ds[part, :], keys), dq)
            dk = jnp.where(here, dks[part, :], dk)
            dv = jnp.where(here, dvs[part, :], dv)
        dqkv_ref[:, at : at + LANES] = (dq * scale).astype(BF16)
        dqkv_ref[:, width + at : width + at + LANES] = (dk * scale).astype(BF16)
        dqkv_ref[:, 2 * width + at : 2 * width + at + LANES] = dv.astype(BF16)
    x = jnp.concatenate([ref[...] for ref in xs], axis=0).astype(F32)
    xhat, rstd = norm_stats(x)
    gain = vector(vecs, GAIN1)
    n1 = (xhat * gain + vector(vecs, BIAS1)).astype(BF16)
    weight_grad(keep_ref, send_ref, core, place, depth, order, proj, 0, n1, dqkv_ref)
    dn1 = dot_nt(dqkv_ref[...], w_qkv[...])
    dx = (dx2_ref[...] + norm_back(dn1, xhat, rstd, gain)).astype(BF16)
    d_mask = jnp.zeros((16, width), F32)
    for k in range(count):
        part = dx[k * share : (k + 1) * share, :]
        d_mask = d_mask + dot(cs[k][share : share + 16, :share], part)
        ref, at = results[min(k, 2)], 2 * share * max(k - 2, 0)
        ref[at : at + share, :] = block_ref[k * share : (k + 1) * share, :]
        ref[at + share : at + 2 * share, :] = part
    blocks = small.shape[0]
    small[...] = jnp.zeros(small.shape, F32)
    wide = [
        d_mask[0:1, :],
        jnp.sum(dn1 * xhat, axis=0, keepdims=True),
        jnp.sum(dn1, axis=0, keepdims=True),
        jnp.sum(dqkv_ref[:, :width].astype(F32), axis=0, keepdims=True),
        jnp.sum(dqkv_ref[:, 2 * width :].astype(F32), axis=0, keepdims=True),
        sub_ref[1:2, :],
        sub_ref[0:1, :],
    ]
    lines = [v[:, j : j + LANES] for v in wide for j in range(0, v.shape[1], LANES)]
    each = -(-len(lines) // blocks)
    for i, line in enumerate(lines):
        small[i // each, i % each : i % each + 1, :] = line
    chips = blocks // 2
    for out_ref, owner in ((send_ref, core ^ 1), (keep_ref, core)):
        for index in range(chips):
            rel = relative(owner, place, chip_of(index, depth), depth, order)
            out_ref[rel, proj.tall : proj.tall + 16, :] = small[owner * chips + index].astype(BF16)


def gather_kernel(depth, order, layout, scale, small_at, sizes, *refs):
    count = len(layout)
    halves, outs = refs[:4], refs[4 : 4 + count]
    vectors = refs[4 + count : 4 + count + len(sizes)]
    held = refs[4 + count + len(sizes) : -2]
    small, sems = refs[-2:]
    core, place, _ = place_of()
    half = halves[0].shape[0]
    chips = 2 * half
    copies = []
    for side, owner in ((0, core), (1, core ^ 1)):
        for rel in range(chips):
            ref, at_block = halves[2 * side + rel // half], rel % half
            index = absolute(owner, place, rel, depth, order)
            slot = side * chips + rel
            for which, (pieces, base) in enumerate(layout):
                for j in range(pieces.width // LANES):
                    at = base + j * pieces.height
                    held[which][slot, :, j * LANES : (j + 1) * LANES] = (
                        ref[at_block, at : at + pieces.height, :].astype(F32) * scale
                    )
                top = pl.multiple_of((index // pieces.lane_blocks) * pieces.height, 16)
                lane = owner * pieces.half + (index % pieces.lane_blocks) * pieces.width
                copy = pltpu.make_async_copy(
                    held[which].at[slot],
                    outs[which].at[
                        pl.ds(top, pieces.height),
                        pl.ds(pl.multiple_of(lane, LANES), pieces.width),
                    ],
                    sems.at[which, slot],
                )
                copy.start()
                copies.append(copy)
            if sizes:
                small[owner * chips + index] = (
                    ref[at_block, small_at : small_at + 16, :].astype(F32) * scale
                )
    lines = sum(sizes) // LANES
    each = max(1, -(-lines // (2 * chips)))
    line = 0
    for out, size in zip(vectors, sizes):
        for j in range(size // LANES):
            out[j * LANES : (j + 1) * LANES] = small[
                line // each, line % each : line % each + 1, :
            ].reshape(LANES)
            line += 1
    for copy in copies:
        copy.wait()


def finish_kernel(flags, *refs):
    block_out, token_grad = refs[-2:]
    share = block_out.shape[1]
    blk = lax.axis_index("blk")
    for k, ref in enumerate(refs[:-2]):
        at = blk ^ k
        block_out[at] = ref[:share, :]
        token_grad[at] = jnp.where(
            flag_column(flags, at), 0.0, ref[share : 2 * share, :].astype(F32)
        )


WHOLE = pl.BlockSpec(memory_space=pltpu.VMEM)
FAR = pl.BlockSpec(memory_space=pltpu.HBM)


def call(kernel, outs, *args, scratch=(), far=0, far_outs=0, name=None):
    args = list(args)
    for i in range(far):
        args[i] = pltpu.with_memory_space_constraint(args[i], pltpu.HBM)
    return pl.pallas_call(
        kernel,
        out_shape=tuple(outs),
        in_specs=[FAR] * far + [WHOLE] * (len(args) - far),
        out_specs=tuple([FAR] * far_outs + [WHOLE] * (len(outs) - far_outs)),
        scratch_shapes=list(scratch),
        compiler_params=pltpu.CompilerParams(vmem_limit_bytes=VMEM_LIMIT),
        cost_estimate=pl.CostEstimate(
            flops=int(US.get(name, 0) * 1.15e9), bytes_accessed=0, transcendentals=0
        ),
        name=name,
    )(*args)


def like(array):
    return pltpu.VMEM(array.shape, array.dtype)


def after(value, *others):
    return lax.optimization_barrier((value, *others))[0]


def shape(dims, kind=BF16):
    return jax.ShapeDtypeStruct(tuple(dims), kind)


def add(*parts):
    total = parts[0].astype(F32)
    for part in parts[1:]:
        total = total + part.astype(F32)
    return total.astype(BF16)


def shards(
    dp_size,
    blk_size,
    tokens,
    mask_flags,
    buckets,
    cotangent,
    mask_token,
    norm1_gain,
    norm1_bias,
    w_qkv,
    b_query,
    b_value,
    w_out,
    b_out,
    norm2_gain,
    norm2_bias,
    w_up,
    b_up,
    w_down,
    b_down,
):
    micro_count, images, share, width = tokens.shape
    hidden = w_up.shape[1]
    count = micro_count * images
    rows = count * share
    deep = dp_size // 2
    depth = deep // 2
    chips = 4 * depth
    total_images = float(micro_count * images * dp_size)

    def send(value, change):
        table = []
        for d in range(dp_size):
            for b in range(blk_size):
                nz, ny, nx, nc = change(d // 2, d % 2, b // 2, b % 2)
                table.append((d * blk_size + b, (nz * 2 + ny) * blk_size + nx * 2 + nc))
        return lax.ppermute(value, ("dp", "blk"), table)

    def core_pair(z, y, x, c):
        return z, y, x, c ^ 1

    def depth_pair(k):
        return lambda z, y, x, c: (z ^ k, y, x, c)

    def image_pair(k):
        return lambda z, y, x, c: (z, y, x ^ (k >> 1), c ^ (k & 1))

    def halving(order):
        def flip(bits):
            def change(z, y, x, c):
                axis, bit = bits[c]
                at = {"z": z, "y": y, "x": x}
                at[axis] ^= bit
                return at["z"], at["y"], at["x"], c

            return change

        return [flip(bits) for bits in zip(*exchanges(order, depth))]

    class Sum:
        def __init__(self, keep, sent, order):
            self.order = order
            self.pairs = halving(order)
            self.keep, self.sent = keep, sent
            self.step = 0

        def cores(self, *behind):
            self.got = send(after(self.sent, *behind) if behind else self.sent, core_pair)
            return self

        def advance(self, *behind):
            count = len(self.pairs)
            if self.step < count:
                half = self.keep.shape[0] // 2
                away = add(self.keep[half:], self.got[half:])
                self.keep = add(self.keep[:half], self.got[:half])
                change = self.pairs[self.step]
            elif self.step == count:
                away = self.keep = add(self.keep, self.got)
                change = depth_pair(depth)
            else:
                if self.step == count + 1:
                    self.keep = add(self.keep, self.got)
                else:
                    self.keep = jnp.concatenate([self.keep, self.got])
                away = self.keep
                change = self.pairs[2 * count - self.step]
            self.got = send(after(away, *behind) if behind else away, change)
            self.step += 1

        @property
        def left(self):
            return 2 * len(self.pairs) + 1 - self.step

        def finish(self):
            mine = (self.keep, self.got)
            return mine + tuple(send(a, core_pair) for a in mine)

    down = Pieces(hidden, width, chips)
    up = Pieces(width, hidden, chips)
    out = Pieces(width, width, chips)
    proj = Pieces(width, 3 * width, chips)
    dma = pltpu.SemaphoreType.DMA

    tokens_in = tokens.reshape(count, share, width)
    flags = mask_flags.reshape(count, 1, share)
    cots_in = cotangent.reshape(count, share, width)
    filled = call(
        functools.partial(fill_kernel, count),
        [shape((share, width))] * count + [shape((share + 16, width))] * count,
        tokens_in,
        cots_in,
        flags,
        mask_token,
        far=4,
        scratch=[like(tokens_in), like(cots_in), like(flags), like(mask_token), dma((4,))],
        name="fill",
    )
    xs = list(filled[:1]) + [send(filled[k], image_pair(k)) for k in range(1, count)]
    cs = [filled[count]] + [
        send(after(filled[count + k], xs[1]), image_pair(k)) for k in range(1, count)
    ]
    vectors = [norm1_gain, norm1_bias, b_query, b_value, b_out, norm2_gain, norm2_bias, b_down, b_up]
    w_qkv, vecs = call(
        functools.partial(prefetch_kernel, images),
        [shape(w_qkv.shape), shape((16, width), F32)],
        after(w_qkv, xs[1]),
        buckets.T,
        *vectors,
        far=2 + len(vectors),
        scratch=[like(v) for v in vectors] + [like(buckets.T), dma((2 + len(vectors),))],
        name="prefetch",
    )
    weights = [w_out, w_up, w_down]
    w_out, w_up, w_down, qkv, p, rinv, o, x2, n2, h, gp = call(
        functools.partial(forward_kernel, count, share),
        [shape(w.shape) for w in weights]
        + [
            shape((rows, 3 * width)),
            shape((HEADS, rows, rows)),
            shape((rows, width), F32),
            shape((rows, width)),
            shape((rows, width), F32),
            shape((rows, width)),
            shape((rows, hidden)),
            shape((rows, hidden)),
        ],
        *weights,
        *xs,
        vecs,
        w_qkv,
        far=len(weights),
        scratch=[dma((len(weights),))],
        name="forward",
    )
    g, keep, sent = call(
        functools.partial(down_kernel, depth, ORDERS[0], down, count, share),
        [shape((rows, width))] + [shape((chips, down.tall, LANES))] * 2,
        *cs,
        vecs,
        h,
        name="down",
    )
    one = Sum(keep, sent, ORDERS[0]).cores()
    keep, sent, dx2, dx2r, block, sub = call(
        functools.partial(middle_kernel, depth, ORDERS[1], up, out),
        [shape((chips, up.tall + out.tall, LANES))] * 2
        + [
            shape((rows, width), F32),
            shape((rows, width)),
            shape((rows, width)),
            shape((8, hidden), F32),
        ],
        g,
        gp,
        h,
        n2,
        o,
        x2,
        vecs,
        w_up,
        w_down,
        scratch=[pltpu.VMEM((rows, hidden), BF16)],
        name="middle",
    )
    two = Sum(keep, sent, ORDERS[1]).cores()
    early = [one.got, two.got][:BEFORE]
    if early:
        dx2r = after(dx2r, *early)
    one.advance()
    *results, keep, sent = call(
        functools.partial(backward_kernel, depth, ORDERS[2], proj, count, share),
        [shape((2 * share, width))] * 2
        + [shape((2 * share * (count - 2), width))]
        + [shape((chips, proj.tall + 16, LANES))] * 2,
        *xs,
        *cs,
        qkv,
        p,
        rinv,
        o,
        dx2,
        dx2r,
        block,
        sub,
        vecs,
        w_qkv,
        w_out,
        scratch=[
            pltpu.VMEM((rows, 3 * width), BF16),
            pltpu.VMEM((2 * chips, 16, LANES), F32),
        ],
        name="backward",
    )
    three = Sum(keep, sent, ORDERS[2])
    three.cores(*[two.got][:THIRD])
    def whole(group, layout, small_at=0, sizes=(), name=None):
        outs = [shape((p.rows, 2 * p.half), F32) for p, _ in layout]
        outs += [shape((n,), F32) for n in sizes]
        return call(
            functools.partial(
                gather_kernel, depth, group.order, layout, 1.0 / total_images, small_at, sizes
            ),
            outs,
            *group.finish(),
            far_outs=len(layout),
            scratch=[pltpu.VMEM((2 * chips, p.height, p.width), F32) for p, _ in layout]
            + [pltpu.VMEM((2 * chips, 16, LANES), F32), dma((len(layout), 2 * chips))],
            name=name,
        )

    groups = (one, two, three)
    layouts = ([(down, 0)], [(up, 0), (out, up.tall)], [(proj, 0)])
    names = ("gather_down", "gather_up", "gather_proj")
    sizes = (width,) * 9 + (hidden,)
    done = {(3, 0): keep, (0, 0): one.got}
    grads = {}
    progress = True
    while progress:
        progress = False
        for which in (2, 1, 0):
            group = groups[which]
            if which in grads:
                continue
            waits = [b for a, b in TIES if a == (which, group.step)]
            waits += [(4, b) for a, b in WRITTEN if a == (which, group.step)]
            if any(w not in done for w in waits):
                continue
            progress = True
            behind = [done[w] for w in waits]
            if group.left:
                group.advance(*behind)
                done[which, group.step - 1] = group.got
            else:
                if behind:
                    group.got = after(group.got, *behind)
                grads[which] = whole(
                    group,
                    layouts[which],
                    proj.tall if which == 2 else 0,
                    sizes if which == 2 else (),
                    name=names[which],
                )
                done[4, which] = grads[which][0]
        if (5, 0) not in done and RESULTS in done:
            own, near, far = results
            far = send(after(far, done[RESULTS]), image_pair(2))
            near = send(after(near, done[RESULTS]), image_pair(1))
            results = [own, near, far, send(far[2 * share :], image_pair(1))]
            done[5, 0] = results[-1]
            block_out, token_grad = call(
                finish_kernel,
                [shape((count, share, width)), shape((count, share, width), F32)],
                flags,
                *results,
                name="finish",
            )
            done[7, 0] = block_out
            progress = True
    (grad_down,), (grad_up, grad_out), (grad_proj, *small) = (grads[i] for i in range(3))
    mask_g, gain1_g, bias1_g, query_g, value_g, after_g, gain2_g, bias2_g, reduce_g, expand_g = small

    return (
        block_out.reshape(tokens.shape),
        token_grad.reshape(tokens.shape),
        mask_g,
        gain1_g,
        bias1_g,
        grad_proj,
        query_g,
        value_g,
        grad_out,
        after_g,
        gain2_g,
        bias2_g,
        grad_up,
        expand_g,
        grad_down,
        reduce_g,
    )


def solution(mesh):
    rows = P(None, "dp", "blk", None)
    placed = (rows, P(None, "dp", "blk"), P(None, "dp"), rows) + (P(),) * 14
    return jax.shard_map(
        functools.partial(shards, mesh.shape["dp"], mesh.shape["blk"]),
        mesh=mesh,
        in_specs=placed,
        out_specs=(rows, rows) + (P(),) * 14,
        check_vma=False,
    )
```

```python
import functools

import jax
import jax.numpy as jnp
from jax import lax
from jax.experimental import pallas as pl
from jax.experimental.pallas import tpu as pltpu
from jax.sharding import PartitionSpec as P

HEADS = 16
LANES = 128
EPS = 1e-06
LOG2E = 1.4426950408889634
BF16 = jnp.bfloat16
F32 = jnp.float32
ORDERS = (('zxy', 'yxz'), ('yzx', 'zxy'), ('yzx', 'xzy'))
TIES = (((2, 2), (5, 0)), ((0, 2), (1, 0)), ((1, 3), (0, 1)), ((0, 1), (3, 0)), ((2, 4), (1, 4)), ((0, 6), (1, 5)), ((2, 5), (1, 2)), ((2, 1), (3, 0)), ((2, 2), (0, 1)), ((0, 2), (3, 0)), ((2, 3), (1, 2)), ((1, 0), (3, 0)), ((2, 5), (7, 0)))
RESULTS = (1, 2)
WRITTEN = ()
BEFORE = 1
THIRD = 1
US = {'forward': 15, 'gather_up': 8}
VMEM_LIMIT = 24 * 1024 * 1024


def dot(a, b):
    return jnp.dot(a, b, preferred_element_type=F32)


def dot_nt(a, b):
    return lax.dot_general(a, b, (((1,), (1,)), ((), ())), preferred_element_type=F32)


def dot_tn(a, b):
    return lax.dot_general(a, b, (((0,), (0,)), ((), ())), preferred_element_type=F32)


def row(ref):
    return ref[...].astype(F32).reshape(1, -1)


def norm_stats(rows):
    centre = jnp.mean(rows, axis=-1, keepdims=True)
    centred = rows - centre
    spread = jnp.mean(centred * centred, axis=-1, keepdims=True)
    rstd = lax.rsqrt(spread + EPS)
    return centred * rstd, rstd


def norm_back(grad_normed, xhat, rstd, gain):
    grad_xhat = grad_normed * gain
    first = jnp.mean(grad_xhat, axis=-1, keepdims=True)
    second = jnp.mean(grad_xhat * xhat, axis=-1, keepdims=True)
    return rstd * (grad_xhat - first - xhat * second)


class Pieces:
    def __init__(self, rows, cols, chips):
        self.rows = rows
        self.half = cols // 2
        self.row_blocks = min(chips, rows // 16)
        self.lane_blocks = chips // self.row_blocks
        self.height = rows // self.row_blocks
        self.width = self.half // self.lane_blocks
        self.tall = self.height * self.width // LANES


def exchanges(order, depth):
    deep = [("z", 1 << i) for i in reversed(range(depth.bit_length() - 1))]
    bits = {"x": [("x", 1)], "y": [("y", 1)], "z": deep}
    return [sum((bits[axis] for axis in axes), []) for axes in order]


def relative(core, place, chip, depth, order):
    differ = dict(zip("xyz", (a ^ b for a, b in zip(place, chip))))
    found = []
    for bits in exchanges(order, depth):
        at = 0
        for axis, bit in bits:
            at = at * 2 + ((differ[axis] & bit) // bit)
        found.append(at)
    return jnp.where(core == 0, *found)


def chip_of(index, depth):
    return index // (2 * depth), (index // depth) % 2, index % depth


def absolute(core, place, index, depth, order):
    flips = []
    for bits in exchanges(order, depth):
        flip = dict.fromkeys("xyz", 0)
        for i, (axis, bit) in enumerate(reversed(bits)):
            flip[axis] |= bit * ((index >> i) & 1)
        flips.append(flip)
    x, y, z = (
        at ^ jnp.where(core == 0, flips[0][axis], flips[1][axis]) for axis, at in zip("xyz", place)
    )
    return (x * 2 + y) * depth + z % depth


def store_pieces(out_ref, core, place, depth, order, pieces, base, value, row_start):
    for first in range(0, value.shape[0], pieces.height):
        row_block = (row_start + first) // pieces.height
        for lane_block in range(pieces.lane_blocks):
            index = row_block * pieces.lane_blocks + lane_block
            rel = relative(core, place, chip_of(index, depth), depth, order)
            for j in range(pieces.width // LANES):
                at = base + j * pieces.height
                lane = lane_block * pieces.width + j * LANES
                out_ref[rel, at : at + pieces.height, :] = value[
                    first : first + pieces.height, lane : lane + LANES
                ].astype(BF16)


def weight_grad(keep_ref, send_ref, core, place, depth, order, pieces, base, lhs, rhs_ref):
    stripe = max(pieces.height, min(256, pieces.rows))
    sides = ((send_ref, core ^ 1), (keep_ref, core))
    rhs = jnp.concatenate(
        [
            rhs_ref[:, pl.ds(pl.multiple_of(owner * pieces.half, LANES), pieces.half)]
            for _, owner in sides
        ],
        axis=1,
    )
    for start in range(0, pieces.rows, stripe):
        value = dot_tn(lhs[:, start : start + stripe], rhs)
        for side, (out_ref, owner) in enumerate(sides):
            part = value[:, side * pieces.half : (side + 1) * pieces.half]
            store_pieces(out_ref, owner, place, depth, order, pieces, base, part, start)


def place_of():
    dp, blk = lax.axis_index("dp"), lax.axis_index("blk")
    return blk % 2, (blk // 2, dp % 2, dp // 2), blk


def fetch(sems, *pairs):
    copies = [pltpu.make_async_copy(a, b, sems.at[i]) for i, (a, b) in enumerate(pairs)]
    for copy in copies:
        copy.start()
    return [copy.wait for copy in copies]


def flag_column(flags, at):
    share = flags.shape[2]
    eye = lax.broadcasted_iota(jnp.int32, (share, share), 0) == lax.broadcasted_iota(
        jnp.int32, (share, share), 1
    )
    return jnp.sum(jnp.where(eye, flags[at], 0), axis=1, keepdims=True) == 1


def fill_kernel(count, tokens_hbm, cotangent_hbm, flags_hbm, mask_hbm, *refs):
    outs, cots = refs[:count], refs[count : 2 * count]
    tokens, cotangent, flags, mask_token, sems = refs[2 * count :]
    waits = fetch(
        sems,
        (tokens_hbm, tokens),
        (flags_hbm, flags),
        (mask_hbm, mask_token),
        (cotangent_hbm, cotangent),
    )
    for wait in waits[:3]:
        wait()
    blk = lax.axis_index("blk")
    share = tokens.shape[1]
    for k in range(count):
        at = blk ^ k
        outs[k][...] = jnp.where(
            flag_column(flags, at), row(mask_token), tokens[at].astype(F32)
        ).astype(BF16)
    waits[3]()
    for k in range(count):
        at = blk ^ k
        cots[k][:share, :] = cotangent[at]
        cots[k][share:, :] = jnp.zeros((16, cots[k].shape[1]), BF16)
        first = lax.broadcasted_iota(jnp.int32, (16, share), 0) == 0
        flag = (flags[at] == 1).astype(F32)
        cots[k][share:, :share] = jnp.where(first, flag, 0.0).astype(BF16)


GAIN1, BIAS1, B_QUERY, B_VALUE, B_OUT, GAIN2, BIAS2, B_DOWN, B_UP = range(9)
QUOTA = 15


def prefetch_kernel(images, weight_hbm, buckets_hbm, *refs):
    count = (len(refs) - 4) // 2
    weight, vecs = refs[count : count + 2]
    held, buckets, sems = refs[count + 2 : -2], refs[-2], refs[-1]
    waits = fetch(
        sems, (weight_hbm, weight), (buckets_hbm, buckets), *zip(refs[:count], held)
    )
    for wait in waits[1:]:
        wait()
    width = vecs.shape[1]
    vecs[...] = jnp.zeros(vecs.shape, F32)
    line = 0
    for ref in held:
        for at in range(0, ref.shape[0], width):
            vecs[line : line + 1, :] = row(ref)[:, at : at + width]
            line += 1
    micro = lax.axis_index("blk") // images
    quota = jnp.zeros((1, 1), jnp.int32)
    for m in range(buckets.shape[1]):
        bucket = buckets[:, m : m + 1]
        here = jnp.where(bucket == 0, 25, jnp.where(bucket == 1, 49, 64))
        quota = quota + jnp.where(micro == m, here, 0)
    vecs[QUOTA : QUOTA + 1, :] = jnp.broadcast_to(quota.astype(F32), (1, width))
    waits[0]()


def vector(rows, which):
    return rows[which : which + 1, :]


def forward_kernel(count, share, *refs):
    sources, refs = refs[:3], refs[3:]
    xs, refs = refs[:count], refs[count:]
    vecs, w_qkv = refs[:2]
    targets = refs[2:5]
    qkv_ref, p_ref, rinv_ref, o_ref, x2_ref, n2_ref, h_ref, gp_ref, sems = refs[5:]
    waits = fetch(sems, *zip(sources, targets))
    w_out, w_up, _ = targets
    quota = vecs[QUOTA : QUOTA + 1, 0:1].astype(jnp.int32)
    width = xs[0].shape[1]
    head = width // HEADS
    rows = count * share
    x = jnp.concatenate([ref[...] for ref in xs], axis=0).astype(F32)
    xhat, _ = norm_stats(x)
    n1 = (xhat * vector(vecs, GAIN1) + vector(vecs, BIAS1)).astype(BF16)
    for part in range(3):
        cols = slice(part * width, (part + 1) * width)
        value = dot(n1, w_qkv[:, cols])
        if part == 0:
            value = value + vector(vecs, B_QUERY)
        if part == 2:
            value = value + vector(vecs, B_VALUE)
        qkv_ref[:, cols] = value.astype(BF16)
    key = lax.broadcasted_iota(jnp.int32, (rows, 1), 0)
    dead = jnp.where(key % share < quota, 0.0, -1e30).astype(F32)
    lane_head = lax.broadcasted_iota(jnp.int32, (1, LANES), 1) // head
    scale = head ** (-0.5) * LOG2E
    per = LANES // head
    ones = jnp.ones((rows, LANES), BF16)
    for group in range(width // LANES):
        at = group * LANES
        q = qkv_ref[:, at : at + LANES]
        keys = qkv_ref[:, width + at : width + at + LANES]
        values = jnp.concatenate(
            [qkv_ref[:, 2 * width + at : 2 * width + at + LANES], ones], axis=1
        )
        acc = jnp.zeros((rows, LANES), F32)
        racc = jnp.zeros((rows, LANES), F32)
        stack = jnp.concatenate(
            [keys * (lane_head == i).astype(F32).astype(BF16) for i in range(per)], axis=0
        )
        scores = dot_nt(stack, q)
        for i in range(per):
            here = lane_head == i
            s = scores[i * rows : (i + 1) * rows, :] * scale + dead
            top = jnp.max(s, axis=0, keepdims=True)
            p = jnp.exp2(s - top).astype(BF16)
            p_ref[group * per + i] = p
            both = dot_tn(p, values)
            rinv = 1.0 / both[:, LANES:]
            acc = jnp.where(here, both[:, :LANES] * rinv, acc)
            racc = jnp.where(here, rinv, racc)
        o_ref[:, at : at + LANES] = acc.astype(BF16)
        rinv_ref[:, at : at + LANES] = racc
    waits[0]()
    x2 = x + (dot(o_ref[...], w_out[...]) + vector(vecs, B_OUT))
    x2_ref[...] = x2
    xhat2, _ = norm_stats(x2)
    n2 = (xhat2 * vector(vecs, GAIN2) + vector(vecs, BIAS2)).astype(BF16)
    n2_ref[...] = n2
    hidden = w_up.shape[1]
    step = width
    waits[1]()
    for start in range(0, hidden, step):
        cols = slice(start, start + step)
        u = dot(n2, w_up[:, cols]) + vector(vecs, B_UP + start // step)
        cdf = 0.5 + 0.5 * lax.erf(u * (0.5**0.5))
        pdf = jnp.exp(-0.5 * u * u) * 0.3989422804014327
        h_ref[:, cols] = (u * cdf).astype(BF16)
        gp_ref[:, cols] = (cdf + u * pdf).astype(BF16)
    waits[2]()


def down_kernel(depth, order, down, count, share, *refs):
    cs, (vecs, h_ref, g_ref, keep_ref, send_ref) = refs[:count], refs[count:]
    core, place, _ = place_of()
    quota = vecs[QUOTA : QUOTA + 1, 0:1].astype(jnp.int32)
    live_rows = lax.broadcasted_iota(jnp.int32, (share, 1), 0) < quota
    for k in range(count):
        g_ref[k * share : (k + 1) * share, :] = jnp.where(
            live_rows, cs[k][:share, :].astype(F32), 0.0
        ).astype(BF16)
    weight_grad(keep_ref, send_ref, core, place, depth, order, down, 0, h_ref, g_ref)


def middle_kernel(
    depth,
    order,
    up,
    after,
    g_ref, gp_ref, h_ref, n2_ref, o_ref, x2_ref, vecs, w_up, w_down,
    keep_ref, send_ref, dx2_ref, dx2r_ref, out_ref, small_ref, du_ref,
):
    core, place, _ = place_of()
    g = g_ref[...]
    hidden = w_up.shape[1]
    width = g.shape[1]
    step = 512
    small_ref[...] = jnp.zeros(small_ref.shape, F32)
    dn2 = jnp.zeros((g.shape[0], width), F32)
    for start in range(0, hidden, step):
        cols = slice(start, start + step)
        dh = dot_nt(g, w_down[cols, :])
        du = (dh * gp_ref[:, cols].astype(F32)).astype(BF16)
        du_ref[:, cols] = du
        small_ref[0:1, cols] = jnp.sum(du.astype(F32), axis=0, keepdims=True)
        dn2 = dn2 + dot_nt(du, w_up[:, cols])
    x2 = x2_ref[...]
    xhat, rstd = norm_stats(x2)
    gf = g.astype(F32)
    dx2 = gf + norm_back(dn2, xhat, rstd, vector(vecs, GAIN2))
    dx2_ref[...] = dx2
    dx2r = dx2.astype(BF16)
    dx2r_ref[...] = dx2r
    small_ref[1:2, 0:width] = jnp.sum(dx2r.astype(F32), axis=0, keepdims=True)
    small_ref[1:2, width : 2 * width] = jnp.sum(dn2 * xhat, axis=0, keepdims=True)
    small_ref[1:2, 2 * width : 3 * width] = jnp.sum(dn2, axis=0, keepdims=True)
    small_ref[1:2, 3 * width : 4 * width] = jnp.sum(gf, axis=0, keepdims=True)
    weight_grad(keep_ref, send_ref, core, place, depth, order, up, 0, n2_ref, du_ref)
    weight_grad(keep_ref, send_ref, core, place, depth, order, after, up.tall, o_ref, dx2r_ref)
    out_ref[...] = (x2 + (dot(h_ref[...], w_down[...]) + vector(vecs, B_DOWN))).astype(BF16)


def backward_kernel(
    depth,
    order,
    proj,
    count,
    share,
    *refs,
):
    refs = list(refs)
    xs = [refs.pop(0) for _ in range(count)]
    cs = [refs.pop(0) for _ in range(count)]
    qkv_ref, p_ref, rinv_ref, o_ref, dx2_ref, dx2r_ref, block_ref, sub_ref, vecs, w_qkv, w_out = refs[:11]
    refs = refs[11:]
    results = [refs.pop(0) for _ in range(3)]
    keep_ref, send_ref, dqkv_ref, small = refs
    core, place, _ = place_of()
    rows = count * share
    width = xs[0].shape[1]
    head = width // HEADS
    per = LANES // head
    d_o = dot_nt(dx2r_ref[...], w_out[...]).astype(BF16).astype(F32)
    d_scaled = d_o * rinv_ref[...]
    product = (d_scaled * o_ref[...].astype(F32)).astype(BF16)
    d_scaled = d_scaled.astype(BF16)
    lane_head = lax.broadcasted_iota(jnp.int32, (1, LANES), 1) // head
    minus = jnp.full((rows, LANES), -1.0, BF16)
    scale = head ** (-0.5)
    for group in range(width // LANES):
        at = group * LANES
        q = qkv_ref[:, at : at + LANES]
        keys = qkv_ref[:, width + at : width + at + LANES]
        values = qkv_ref[:, 2 * width + at : 2 * width + at + LANES]
        ds_o = d_scaled[:, at : at + LANES]
        rhs = jnp.concatenate([ds_o, product[:, at : at + LANES]], axis=1)
        dq = jnp.zeros((rows, LANES), F32)
        dk = jnp.zeros((rows, LANES), F32)
        dv = jnp.zeros((rows, LANES), F32)
        stack = jnp.concatenate(
            [
                jnp.concatenate(
                    [
                        values * (lane_head == i).astype(F32).astype(BF16),
                        minus * (lane_head == i).astype(F32).astype(BF16),
                    ],
                    axis=1,
                )
                for i in range(per)
            ],
            axis=0,
        )
        p = p_ref[group * per : (group + 1) * per].reshape(per * rows, rows)
        ds = (p.astype(F32) * dot_nt(stack, rhs)).astype(BF16)
        dks = dot(ds, q)
        dvs = dot(p, ds_o)
        for i in range(per):
            here = lane_head == i
            part = slice(i * rows, (i + 1) * rows)
            dq = jnp.where(here, dot_tn(ds[part, :], keys), dq)
            dk = jnp.where(here, dks[part, :], dk)
            dv = jnp.where(here, dvs[part, :], dv)
        dqkv_ref[:, at : at + LANES] = (dq * scale).astype(BF16)
        dqkv_ref[:, width + at : width + at + LANES] = (dk * scale).astype(BF16)
        dqkv_ref[:, 2 * width + at : 2 * width + at + LANES] = dv.astype(BF16)
    x = jnp.concatenate([ref[...] for ref in xs], axis=0).astype(F32)
    xhat, rstd = norm_stats(x)
    gain = vector(vecs, GAIN1)
    n1 = (xhat * gain + vector(vecs, BIAS1)).astype(BF16)
    weight_grad(keep_ref, send_ref, core, place, depth, order, proj, 0, n1, dqkv_ref)
    dn1 = dot_nt(dqkv_ref[...], w_qkv[...])
    dx = (dx2_ref[...] + norm_back(dn1, xhat, rstd, gain)).astype(BF16)
    d_mask = jnp.zeros((16, width), F32)
    for k in range(count):
        part = dx[k * share : (k + 1) * share, :]
        d_mask = d_mask + dot(cs[k][share : share + 16, :share], part)
        ref, at = results[min(k, 2)], 2 * share * max(k - 2, 0)
        ref[at : at + share, :] = block_ref[k * share : (k + 1) * share, :]
        ref[at + share : at + 2 * share, :] = part
    blocks = small.shape[0]
    small[...] = jnp.zeros(small.shape, F32)
    wide = [
        d_mask[0:1, :],
        jnp.sum(dn1 * xhat, axis=0, keepdims=True),
        jnp.sum(dn1, axis=0, keepdims=True),
        jnp.sum(dqkv_ref[:, :width].astype(F32), axis=0, keepdims=True),
        jnp.sum(dqkv_ref[:, 2 * width :].astype(F32), axis=0, keepdims=True),
        sub_ref[1:2, :],
        sub_ref[0:1, :],
    ]
    lines = [v[:, j : j + LANES] for v in wide for j in range(0, v.shape[1], LANES)]
    each = -(-len(lines) // blocks)
    for i, line in enumerate(lines):
        small[i // each, i % each : i % each + 1, :] = line
    chips = blocks // 2
    for out_ref, owner in ((send_ref, core ^ 1), (keep_ref, core)):
        for index in range(chips):
            rel = relative(owner, place, chip_of(index, depth), depth, order)
            out_ref[rel, proj.tall : proj.tall + 16, :] = small[owner * chips + index].astype(BF16)


def gather_kernel(depth, order, layout, scale, small_at, sizes, *refs):
    count = len(layout)
    halves, outs = refs[:4], refs[4 : 4 + count]
    vectors = refs[4 + count : 4 + count + len(sizes)]
    held = refs[4 + count + len(sizes) : -2]
    small, sems = refs[-2:]
    core, place, _ = place_of()
    half = halves[0].shape[0]
    chips = 2 * half
    copies = []
    for side, owner in ((0, core), (1, core ^ 1)):
        for rel in range(chips):
            ref, at_block = halves[2 * side + rel // half], rel % half
            index = absolute(owner, place, rel, depth, order)
            slot = side * chips + rel
            for which, (pieces, base) in enumerate(layout):
                for j in range(pieces.width // LANES):
                    at = base + j * pieces.height
                    held[which][slot, :, j * LANES : (j + 1) * LANES] = (
                        ref[at_block, at : at + pieces.height, :].astype(F32) * scale
                    )
                top = pl.multiple_of((index // pieces.lane_blocks) * pieces.height, 16)
                lane = owner * pieces.half + (index % pieces.lane_blocks) * pieces.width
                copy = pltpu.make_async_copy(
                    held[which].at[slot],
                    outs[which].at[
                        pl.ds(top, pieces.height),
                        pl.ds(pl.multiple_of(lane, LANES), pieces.width),
                    ],
                    sems.at[which, slot],
                )
                copy.start()
                copies.append(copy)
            if sizes:
                small[owner * chips + index] = (
                    ref[at_block, small_at : small_at + 16, :].astype(F32) * scale
                )
    lines = sum(sizes) // LANES
    each = max(1, -(-lines // (2 * chips)))
    line = 0
    for out, size in zip(vectors, sizes):
        for j in range(size // LANES):
            out[j * LANES : (j + 1) * LANES] = small[
                line // each, line % each : line % each + 1, :
            ].reshape(LANES)
            line += 1
    for copy in copies:
        copy.wait()


def finish_kernel(flags, *refs):
    block_out, token_grad = refs[-2:]
    share = block_out.shape[1]
    blk = lax.axis_index("blk")
    for k, ref in enumerate(refs[:-2]):
        at = blk ^ k
        block_out[at] = ref[:share, :]
        token_grad[at] = jnp.where(
            flag_column(flags, at), 0.0, ref[share : 2 * share, :].astype(F32)
        )


WHOLE = pl.BlockSpec(memory_space=pltpu.VMEM)
FAR = pl.BlockSpec(memory_space=pltpu.HBM)


def call(kernel, outs, *args, scratch=(), far=0, far_outs=0, name=None):
    args = list(args)
    for i in range(far):
        args[i] = pltpu.with_memory_space_constraint(args[i], pltpu.HBM)
    return pl.pallas_call(
        kernel,
        out_shape=tuple(outs),
        in_specs=[FAR] * far + [WHOLE] * (len(args) - far),
        out_specs=tuple([FAR] * far_outs + [WHOLE] * (len(outs) - far_outs)),
        scratch_shapes=list(scratch),
        compiler_params=pltpu.CompilerParams(vmem_limit_bytes=VMEM_LIMIT),
        cost_estimate=pl.CostEstimate(
            flops=int(US.get(name, 0) * 1.15e9), bytes_accessed=0, transcendentals=0
        ),
        name=name,
    )(*args)


def like(array):
    return pltpu.VMEM(array.shape, array.dtype)


def after(value, *others):
    return lax.optimization_barrier((value, *others))[0]


def shape(dims, kind=BF16):
    return jax.ShapeDtypeStruct(tuple(dims), kind)


def add(*parts):
    total = parts[0].astype(F32)
    for part in parts[1:]:
        total = total + part.astype(F32)
    return total.astype(BF16)


def shards(
    dp_size,
    blk_size,
    tokens,
    mask_flags,
    buckets,
    cotangent,
    mask_token,
    norm1_gain,
    norm1_bias,
    w_qkv,
    b_query,
    b_value,
    w_out,
    b_out,
    norm2_gain,
    norm2_bias,
    w_up,
    b_up,
    w_down,
    b_down,
):
    micro_count, images, share, width = tokens.shape
    hidden = w_up.shape[1]
    count = micro_count * images
    rows = count * share
    deep = dp_size // 2
    depth = deep // 2
    chips = 4 * depth
    total_images = float(micro_count * images * dp_size)

    def send(value, change):
        table = []
        for d in range(dp_size):
            for b in range(blk_size):
                nz, ny, nx, nc = change(d // 2, d % 2, b // 2, b % 2)
                table.append((d * blk_size + b, (nz * 2 + ny) * blk_size + nx * 2 + nc))
        return lax.ppermute(value, ("dp", "blk"), table)

    def core_pair(z, y, x, c):
        return z, y, x, c ^ 1

    def depth_pair(k):
        return lambda z, y, x, c: (z ^ k, y, x, c)

    def image_pair(k):
        return lambda z, y, x, c: (z, y, x ^ (k >> 1), c ^ (k & 1))

    def halving(order):
        def flip(bits):
            def change(z, y, x, c):
                axis, bit = bits[c]
                at = {"z": z, "y": y, "x": x}
                at[axis] ^= bit
                return at["z"], at["y"], at["x"], c

            return change

        return [flip(bits) for bits in zip(*exchanges(order, depth))]

    class Sum:
        def __init__(self, keep, sent, order):
            self.order = order
            self.pairs = halving(order)
            self.keep, self.sent = keep, sent
            self.step = 0

        def cores(self, *behind):
            self.got = send(after(self.sent, *behind) if behind else self.sent, core_pair)
            return self

        def advance(self, *behind):
            count = len(self.pairs)
            if self.step < count:
                half = self.keep.shape[0] // 2
                away = add(self.keep[half:], self.got[half:])
                self.keep = add(self.keep[:half], self.got[:half])
                change = self.pairs[self.step]
            elif self.step == count:
                away = self.keep = add(self.keep, self.got)
                change = depth_pair(depth)
            else:
                if self.step == count + 1:
                    self.keep = add(self.keep, self.got)
                else:
                    self.keep = jnp.concatenate([self.keep, self.got])
                away = self.keep
                change = self.pairs[2 * count - self.step]
            self.got = send(after(away, *behind) if behind else away, change)
            self.step += 1

        @property
        def left(self):
            return 2 * len(self.pairs) + 1 - self.step

        def finish(self):
            mine = (self.keep, self.got)
            return mine + tuple(send(a, core_pair) for a in mine)

    down = Pieces(hidden, width, chips)
    up = Pieces(width, hidden, chips)
    out = Pieces(width, width, chips)
    proj = Pieces(width, 3 * width, chips)
    dma = pltpu.SemaphoreType.DMA

    tokens_in = tokens.reshape(count, share, width)
    flags = mask_flags.reshape(count, 1, share)
    cots_in = cotangent.reshape(count, share, width)
    filled = call(
        functools.partial(fill_kernel, count),
        [shape((share, width))] * count + [shape((share + 16, width))] * count,
        tokens_in,
        cots_in,
        flags,
        mask_token,
        far=4,
        scratch=[like(tokens_in), like(cots_in), like(flags), like(mask_token), dma((4,))],
        name="fill",
    )
    xs = list(filled[:1]) + [send(filled[k], image_pair(k)) for k in range(1, count)]
    cs = [filled[count]] + [
        send(after(filled[count + k], xs[1]), image_pair(k)) for k in range(1, count)
    ]
    vectors = [norm1_gain, norm1_bias, b_query, b_value, b_out, norm2_gain, norm2_bias, b_down, b_up]
    w_qkv, vecs = call(
        functools.partial(prefetch_kernel, images),
        [shape(w_qkv.shape), shape((16, width), F32)],
        after(w_qkv, xs[1]),
        buckets.T,
        *vectors,
        far=2 + len(vectors),
        scratch=[like(v) for v in vectors] + [like(buckets.T), dma((2 + len(vectors),))],
        name="prefetch",
    )
    weights = [w_out, w_up, w_down]
    w_out, w_up, w_down, qkv, p, rinv, o, x2, n2, h, gp = call(
        functools.partial(forward_kernel, count, share),
        [shape(w.shape) for w in weights]
        + [
            shape((rows, 3 * width)),
            shape((HEADS, rows, rows)),
            shape((rows, width), F32),
            shape((rows, width)),
            shape((rows, width), F32),
            shape((rows, width)),
            shape((rows, hidden)),
            shape((rows, hidden)),
        ],
        *weights,
        *xs,
        vecs,
        w_qkv,
        far=len(weights),
        scratch=[dma((len(weights),))],
        name="forward",
    )
    g, keep, sent = call(
        functools.partial(down_kernel, depth, ORDERS[0], down, count, share),
        [shape((rows, width))] + [shape((chips, down.tall, LANES))] * 2,
        *cs,
        vecs,
        h,
        name="down",
    )
    one = Sum(keep, sent, ORDERS[0]).cores()
    keep, sent, dx2, dx2r, block, sub = call(
        functools.partial(middle_kernel, depth, ORDERS[1], up, out),
        [shape((chips, up.tall + out.tall, LANES))] * 2
        + [
            shape((rows, width), F32),
            shape((rows, width)),
            shape((rows, width)),
            shape((8, hidden), F32),
        ],
        g,
        gp,
        h,
        n2,
        o,
        x2,
        vecs,
        w_up,
        w_down,
        scratch=[pltpu.VMEM((rows, hidden), BF16)],
        name="middle",
    )
    two = Sum(keep, sent, ORDERS[1]).cores()
    early = [one.got, two.got][:BEFORE]
    if early:
        dx2r = after(dx2r, *early)
    one.advance()
    *results, keep, sent = call(
        functools.partial(backward_kernel, depth, ORDERS[2], proj, count, share),
        [shape((2 * share, width))] * 2
        + [shape((2 * share * (count - 2), width))]
        + [shape((chips, proj.tall + 16, LANES))] * 2,
        *xs,
        *cs,
        qkv,
        p,
        rinv,
        o,
        dx2,
        dx2r,
        block,
        sub,
        vecs,
        w_qkv,
        w_out,
        scratch=[
            pltpu.VMEM((rows, 3 * width), BF16),
            pltpu.VMEM((2 * chips, 16, LANES), F32),
        ],
        name="backward",
    )
    three = Sum(keep, sent, ORDERS[2])
    three.cores(*[two.got][:THIRD])
    def whole(group, layout, small_at=0, sizes=(), name=None):
        outs = [shape((p.rows, 2 * p.half), F32) for p, _ in layout]
        outs += [shape((n,), F32) for n in sizes]
        return call(
            functools.partial(
                gather_kernel, depth, group.order, layout, 1.0 / total_images, small_at, sizes
            ),
            outs,
            *group.finish(),
            far_outs=len(layout),
            scratch=[pltpu.VMEM((2 * chips, p.height, p.width), F32) for p, _ in layout]
            + [pltpu.VMEM((2 * chips, 16, LANES), F32), dma((len(layout), 2 * chips))],
            name=name,
        )

    groups = (one, two, three)
    layouts = ([(down, 0)], [(up, 0), (out, up.tall)], [(proj, 0)])
    names = ("gather_down", "gather_up", "gather_proj")
    sizes = (width,) * 9 + (hidden,)
    done = {(3, 0): keep, (0, 0): one.got}
    grads = {}
    progress = True
    while progress:
        progress = False
        for which in (2, 1, 0):
            group = groups[which]
            if which in grads:
                continue
            waits = [b for a, b in TIES if a == (which, group.step)]
            waits += [(4, b) for a, b in WRITTEN if a == (which, group.step)]
            if any(w not in done for w in waits):
                continue
            progress = True
            behind = [done[w] for w in waits]
            if group.left:
                group.advance(*behind)
                done[which, group.step - 1] = group.got
            else:
                if behind:
                    group.got = after(group.got, *behind)
                grads[which] = whole(
                    group,
                    layouts[which],
                    proj.tall if which == 2 else 0,
                    sizes if which == 2 else (),
                    name=names[which],
                )
                done[4, which] = grads[which][0]
        if (5, 0) not in done and RESULTS in done:
            own, near, far = results
            far = send(after(far, done[RESULTS]), image_pair(2))
            near = send(after(near, done[RESULTS]), image_pair(1))
            results = [own, near, far, send(far[2 * share :], image_pair(1))]
            done[5, 0] = results[-1]
            block_out, token_grad = call(
                finish_kernel,
                [shape((count, share, width)), shape((count, share, width), F32)],
                flags,
                *results,
                name="finish",
            )
            done[7, 0] = block_out
            progress = True
    (grad_down,), (grad_up, grad_out), (grad_proj, *small) = (grads[i] for i in range(3))
    mask_g, gain1_g, bias1_g, query_g, value_g, after_g, gain2_g, bias2_g, reduce_g, expand_g = small

    return (
        block_out.reshape(tokens.shape),
        token_grad.reshape(tokens.shape),
        mask_g,
        gain1_g,
        bias1_g,
        grad_proj,
        query_g,
        value_g,
        grad_out,
        after_g,
        gain2_g,
        bias2_g,
        grad_up,
        expand_g,
        grad_down,
        reduce_g,
    )


def solution(mesh):
    rows = P(None, "dp", "blk", None)
    placed = (rows, P(None, "dp", "blk"), P(None, "dp"), rows) + (P(),) * 14
    return jax.shard_map(
        functools.partial(shards, mesh.shape["dp"], mesh.shape["blk"]),
        mesh=mesh,
        in_specs=placed,
        out_specs=(rows, rows) + (P(),) * 14,
        check_vma=False,
    )
```
